512 devices in a mesh: row: 16 (over x, y), col: 32 (over z, core).
Axes of the slice: x: 4, y: 4, z: 16, core: 2. Of those that a mesh axis runs over, the one named last changes fastest.
Arguments:
- classes: int32 [256, 4096], P('row', 'col'), may hold values from 0 to 15
- check_index: int32 [1], replicated, may hold values from 8 to 64
- saved_snapshot: bfloat16 [24, 256, 4096], P(None, 'row', 'col'), may hold values from -8 to 8
- payoff_map: bfloat16 [24, 256, 4096], P(None, 'row', 'col'), may hold values from -120 to 160
- final_sensitivity: bfloat16 [24, 256, 4096], P(None, 'row', 'col'), may hold values from -36 to 36
- embed: bfloat16 [16, 64], replicated, may hold values from -6 to 6
- time_vec: bfloat16 [64], replicated, may hold values from -6 to 6
- w_one: bfloat16 [64, 64], replicated, may hold values from -0.75 to 0.75
- w_two: bfloat16 [64, 64], replicated, may hold values from -0.75 to 0.75
- w_three: bfloat16 [64, 24], replicated, may hold values from -0.75 to 0.75
Outputs:
- snapshot_sensitivity: bfloat16 [24, 256, 4096], P(None, 'row', 'col')
- payoff_sensitivity: bfloat16 [24, 256, 4096], P(None, 'row', 'col')
- d_embed: float32 [16, 64], replicated
- d_time: float32 [64], replicated
- d_w_one: float32 [64, 64], replicated
- d_w_two: float32 [64, 64], replicated
- d_w_three: float32 [64, 24], replicated
The draws below stay inside these ranges and needn't reach their ends.
All inputs are finite; a program needn't handle non-finite values.
Results may differ from the reference program's by a relative error of at most 0.008.
The reference program's roundings to bfloat16 on the way count: a program that leaves them out, or rounds other values in their place, can miss the bound.
Values may be sent and summed in bfloat16 or wider, within the bound.
No kernel may reach another device: no remote copies, remote signals or barrier semaphores. Data moves between devices by JAX's collectives and lax.ppermute only.
A program may use at most 64 MiB of HBM per device.

```python
import math
import jax
import jax.numpy as jnp
from jax import lax

CR = 16
GOALS = 24
ITERS = 3
CHOICE_NUMBER = 4
STENCIL_POINTS = 5
FEAT = 64
HID = 64
CLASSES = 16
OUTS = 24
NR = 256
NC = 4096


def draw_payoff_map(key, part):
    key = jax.random.fold_in(key, 11)
    key_one = jax.random.fold_in(key, 0)
    full_shape = (GOALS, NR, NC)
    result_map = jnp.clip(2.0 * jax.random.normal(key_one, full_shape, jnp.float32), -12.0, 12.0)
    return result_map.astype(jnp.bfloat16)


def draw_final_sensitivity(key, part):
    key = jax.random.fold_in(key, 23)
    key_one, key_two = jax.random.split(key, 2)
    full_shape = (GOALS, NR, NC)
    col_frac = jnp.arange(NC, dtype=jnp.float32) / NC
    rising = jnp.exp(jnp.log(3.0) * col_frac)
    row_scale = 0.3 * jnp.exp(jax.random.uniform(key_two, (NR,), jnp.float32, 0.0, 2.3026))
    noise_part = jnp.clip(jax.random.normal(key_one, full_shape, jnp.float32), -4.0, 4.0)
    result_map = noise_part * row_scale[None, :, None] * rising[None, None, :]
    return result_map.astype(jnp.bfloat16)


def with_ends(values, own_key, low, largest):
    longest = values.shape.index(max(values.shape))
    spots = []
    for shift in (0, 1):
        where = [jax.random.randint(jax.random.fold_in(own_key, axis), (), 0, length) for axis, length in enumerate(values.shape)]
        where[longest] = (where[longest] + shift) % values.shape[longest]
        spots.append(tuple(where))
    return values.at[spots[0]].set(low).at[spots[1]].set(largest)


def steps_of(stream_key, shape, pieces, smallest, largest):
    loudness, own = 1.0, jax.random.fold_in(stream_key, 6)
    for axis_at, parts in pieces:
        steps = jnp.exp(jax.random.uniform(jax.random.fold_in(own, axis_at), (parts,), jnp.float32, smallest / len(pieces), largest / len(pieces)))
        loudness = loudness * jnp.repeat(steps, shape[axis_at] // parts).reshape([-1 if axis == axis_at else 1 for axis in range(len(shape))])
    return loudness


def normal_values(own_key, extent, spread, bound, pieces=(), kind=jnp.bfloat16):
    gain = steps_of(own_key, extent, pieces, -0.22, 0.18) if pieces else 1.0
    values = jax.random.normal(own_key, extent, jnp.float32) * spread * gain
    return jnp.minimum(jnp.maximum(values, -bound), bound).astype(kind)


def setup_inputs(seed: int = 0) -> dict:
    arg_keys = jax.random.split(jax.random.key(seed), 11)
    return {
        "classes": with_ends(jax.random.randint(arg_keys[0], (NR, NC), 0, CLASSES), jax.random.fold_in(arg_keys[0], 1), 0, CLASSES - 1).astype(jnp.int32),
        "check_index": jax.random.randint(arg_keys[1], (1,), 8, 65).astype(jnp.int32),
        "saved_snapshot": normal_values(arg_keys[2], (GOALS, NR, NC), 2.0, 8.0, ((1, 16), (2, 32))),
        "payoff_map": draw_payoff_map(jax.random.fold_in(arg_keys[10], 71), 0),
        "final_sensitivity": draw_final_sensitivity(jax.random.fold_in(arg_keys[10], 71), 0),
        "embed": normal_values(arg_keys[5], (CLASSES, FEAT), 1.0, 6.0),
        "time_vec": normal_values(arg_keys[6], (FEAT,), 1.0, 6.0),
        "w_one": normal_values(arg_keys[7], (FEAT, HID), FEAT ** -0.5, 0.75),
        "w_two": normal_values(arg_keys[8], (HID, HID), HID ** -0.5, 0.75),
        "w_three": normal_values(arg_keys[9], (HID, OUTS), HID ** -0.5, 0.75),
    }


DECAY_FACTOR = 0.9
SLACK = 0.05

def project(weight_matrix, data_rows):
    return lax.dot_general(weight_matrix, data_rows, (((0,), (0,)), ((), ())), preferred_element_type=jnp.float32)

def contract_cells(first_part, second_part):
    return lax.dot_general(first_part, second_part, (((1,), (1,)), ((), ())), preferred_element_type=jnp.float32)

def network_forward(class_ids, index_scale, embed, time_vec, w_one, w_two, w_three):
    one_hot = (jnp.arange(embed.shape[0], dtype=jnp.int32)[:, None] == class_ids[None, :]).astype(jnp.bfloat16)
    looked = project(embed, one_hot)
    feature = (looked + index_scale * time_vec.astype(jnp.float32)[:, None]).astype(jnp.bfloat16)
    hidden_one = jnp.tanh(project(w_one, feature)).astype(jnp.bfloat16)
    hidden_two = jnp.tanh(project(w_two, hidden_one)).astype(jnp.bfloat16)
    transition_scores = project(w_three, hidden_two)
    return (one_hot, feature, hidden_one, hidden_two, transition_scores)

def blend_weights(transition_scores, widened_height, widened_breadth):
    raw_scores = transition_scores[:CHOICE_NUMBER * STENCIL_POINTS].reshape(CHOICE_NUMBER, STENCIL_POINTS, widened_height, widened_breadth)
    weights = jax.nn.softplus(raw_scores) + SLACK
    normalizer_sums = lax.optimization_barrier(jnp.sum(weights, axis=1, keepdims=True))
    transition_chances = weights / normalizer_sums
    choice_payoff_extra = transition_scores[CHOICE_NUMBER * STENCIL_POINTS:].reshape(CHOICE_NUMBER, widened_height, widened_breadth)
    return (raw_scores, normalizer_sums, transition_chances, choice_payoff_extra)

def neighbours(bordered_worths):
    return (bordered_worths[:, 1:-1, 1:-1], bordered_worths[:, :-2, 1:-1], bordered_worths[:, 2:, 1:-1], bordered_worths[:, 1:-1, :-2], bordered_worths[:, 1:-1, 2:])

def collect_pushed(pushed):
    return pushed[0][:, 1:-1, 1:-1] + pushed[1][:, 2:, 1:-1] + pushed[2][:, :-2, 1:-1] + pushed[3][:, 1:-1, 2:] + pushed[4][:, 1:-1, :-2]

def smooth_bellman_update(bordered_worths, transition_chances, choice_payoff_extra, site_payoff):
    nearby = neighbours(bordered_worths)
    scattered_worths = transition_chances[None, :, 0] * nearby[0][:, None]
    for direction in range(1, STENCIL_POINTS):
        scattered_worths = scattered_worths + transition_chances[None, :, direction] * nearby[direction][:, None]
    quality_table = site_payoff[:, None] + choice_payoff_extra[None] + DECAY_FACTOR * scattered_worths
    highest = lax.optimization_barrier(jnp.max(quality_table, axis=1))
    following_worth = highest + jnp.log(lax.optimization_barrier(jnp.sum(jnp.exp(quality_table - highest[:, None]), axis=1)))
    return (quality_table, following_worth)

def score_sensitivities(chance_sensitivity, extra_payoff_sensitivity, raw_scores, normalizer_sums, transition_chances):
    weighted = lax.optimization_barrier(jnp.sum(chance_sensitivity * transition_chances, axis=1, keepdims=True))
    raw_sensitivity = (chance_sensitivity - weighted) / normalizer_sums * jax.nn.sigmoid(raw_scores)
    lattice_sites = extra_payoff_sensitivity.shape[1] * extra_payoff_sensitivity.shape[2]
    merged_worths = jnp.concatenate([raw_sensitivity.reshape(CHOICE_NUMBER * STENCIL_POINTS, lattice_sites), extra_payoff_sensitivity.reshape(CHOICE_NUMBER, lattice_sites)], axis=0)
    return merged_worths.astype(jnp.bfloat16)

def network_backward(one_hot, feature, hidden_one, hidden_two, score_sensitivity, index_scale, w_one, w_two, w_three):
    grad_three = contract_cells(hidden_two, score_sensitivity)
    two_f = hidden_two.astype(jnp.float32)
    two_grad = (jnp.dot(w_three, score_sensitivity, preferred_element_type=jnp.float32) * (1.0 - two_f * two_f)).astype(jnp.bfloat16)
    grad_two = contract_cells(hidden_one, two_grad)
    one_f = hidden_one.astype(jnp.float32)
    one_grad = (jnp.dot(w_two, two_grad, preferred_element_type=jnp.float32) * (1.0 - one_f * one_f)).astype(jnp.bfloat16)
    grad_one = contract_cells(feature, one_grad)
    feature_grad = jnp.dot(w_one, one_grad, preferred_element_type=jnp.float32).astype(jnp.bfloat16)
    grad_embed = contract_cells(one_hot, feature_grad)
    grad_time = index_scale * lax.optimization_barrier(jnp.sum(feature_grad, axis=1, dtype=jnp.float32))
    return (grad_embed, grad_time, grad_one, grad_two, grad_three)

def reference(classes, check_index, saved_snapshot, payoff_map, final_sensitivity, embed, time_vec, w_one, w_two, w_three):
    bordered_height, bordered_breadth = classes.shape
    index_scale = check_index[0].astype(jnp.float32) / 64.0
    blocks = bordered_height // CR
    class_blocks = classes.reshape(blocks, CR, bordered_breadth)

    def block_logits(class_ids):
        outputs = network_forward(class_ids.reshape(-1), index_scale, embed, time_vec, w_one, w_two, w_three)
        return outputs[4].reshape(OUTS, CR, bordered_breadth)
    transition_scores = lax.map(block_logits, class_blocks)
    transition_scores = jnp.moveaxis(transition_scores, 1, 0).reshape(OUTS, bordered_height * bordered_breadth)
    raw_scores, normalizer_sums, transition_chances, choice_payoff_extra = blend_weights(transition_scores, bordered_height, bordered_breadth)

    def lone_destination(loop_carry, goal_in):
        chance_sensitivity, extra_payoff_sensitivity = loop_carry
        start_map, reward_map, cot_map = goal_in
        site_payoff = reward_map.astype(jnp.float32)[None]
        present_worth = start_map.astype(jnp.float32)[None]
        stored = []
        for iteration in range(ITERS):
            bordered_worths = jnp.pad(present_worth, ((0, 0), (1, 1), (1, 1)))
            stored.append(bordered_worths)
            present_worth = smooth_bellman_update(bordered_worths, transition_chances, choice_payoff_extra, site_payoff)[1]
        worth_sensitivity = cot_map.astype(jnp.float32)[None]
        payoff_site_sensitivity = jnp.zeros_like(worth_sensitivity)
        for iteration in reversed(range(ITERS)):
            bordered_worths = stored[iteration]
            quality_table, following_worth = smooth_bellman_update(bordered_worths, transition_chances, choice_payoff_extra, site_payoff)
            quality_sensitivity = worth_sensitivity[:, None] * jnp.exp(quality_table - following_worth[:, None])
            payoff_site_sensitivity = payoff_site_sensitivity + lax.optimization_barrier(jnp.sum(quality_sensitivity, axis=1))
            extra_payoff_sensitivity = extra_payoff_sensitivity + lax.optimization_barrier(jnp.sum(quality_sensitivity, axis=0))
            nearby = neighbours(bordered_worths)
            chance_sensitivity = chance_sensitivity + DECAY_FACTOR * jnp.stack([lax.optimization_barrier(jnp.sum(quality_sensitivity * nearby[direction][:, None], axis=0)) for direction in range(STENCIL_POINTS)], axis=1)
            pushed = [DECAY_FACTOR * lax.optimization_barrier(jnp.sum(quality_sensitivity * transition_chances[None, :, direction], axis=1)) for direction in range(STENCIL_POINTS)]
            pushed = [jnp.pad(piece, ((0, 0), (1, 1), (1, 1))) for piece in pushed]
            worth_sensitivity = collect_pushed(pushed)
        return ((chance_sensitivity, extra_payoff_sensitivity), (worth_sensitivity[0].astype(jnp.bfloat16), payoff_site_sensitivity[0].astype(jnp.bfloat16)))
    starting_worth = (jnp.zeros((CHOICE_NUMBER, STENCIL_POINTS, bordered_height, bordered_breadth), jnp.float32), jnp.zeros((CHOICE_NUMBER, bordered_height, bordered_breadth), jnp.float32))
    (chance_sensitivity, extra_payoff_sensitivity), (snapshot_sensitivity, payoff_sensitivity) = lax.scan(lone_destination, starting_worth, (saved_snapshot, payoff_map, final_sensitivity))
    score_sensitivity = score_sensitivities(chance_sensitivity, extra_payoff_sensitivity, raw_scores, normalizer_sums, transition_chances)
    grad_blocks = jnp.moveaxis(score_sensitivity.reshape(OUTS, blocks, CR * bordered_breadth), 1, 0)

    def back_block(running, block_in):
        class_ids, block_grad = block_in
        outputs = network_forward(class_ids.reshape(-1), index_scale, embed, time_vec, w_one, w_two, w_three)
        gradients = network_backward(outputs[0], outputs[1], outputs[2], outputs[3], block_grad, index_scale, w_one, w_two, w_three)
        return (tuple((first_part + second_part for first_part, second_part in zip(running, gradients))), None)
    zero_grads = (jnp.zeros(embed.shape, jnp.float32), jnp.zeros(time_vec.shape, jnp.float32), jnp.zeros(w_one.shape, jnp.float32), jnp.zeros(w_two.shape, jnp.float32), jnp.zeros(w_three.shape, jnp.float32))
    summed, unused = lax.scan(back_block, zero_grads, (class_blocks, grad_blocks))
    grad_scale = 1.0 / math.sqrt(bordered_height * bordered_breadth)
    return (snapshot_sensitivity, payoff_sensitivity, summed[0] * grad_scale, summed[1] * grad_scale, summed[2] * grad_scale, summed[3] * grad_scale, summed[4] * grad_scale)
```

```python
import math

import jax
import jax.numpy as jnp
from jax import lax
from jax.experimental import pallas as pl
from jax.experimental.pallas import tpu as pltpu
from jax.sharding import PartitionSpec as P

ITERS = 3
ACTIONS = 4
POINTS = 5
OUTS = 24
GOALS = 24
CLASSES = 16
ROWS = 16
COLS = 128
DECAY = 0.9
SLACK = 0.05
VH, RH, FH = 6, 5, 3
TOP = 16
EXT = 48
GROUP = 16
OCT = GOALS // 8
HIGHEST = lax.Precision.HIGHEST
F32 = jnp.float32
BF16 = jnp.bfloat16


def vmem_call(kernel, out_shape, scratch=(), limit=48 * 1024 * 1024):
    whole = pl.BlockSpec(memory_space=pltpu.VMEM)
    return lambda *args: pl.pallas_call(
        kernel,
        out_shape=out_shape,
        in_specs=[whole] * len(args),
        out_specs=jax.tree.map(lambda _: whole, out_shape),
        scratch_shapes=list(scratch),
        compiler_params=pltpu.CompilerParams(vmem_limit_bytes=limit),
    )(*args)


def lane_iota(shape):
    return lax.broadcasted_iota(jnp.int32, shape, len(shape) - 1)


def turn(x, shift):
    shift = shift % COLS
    return x if shift == 0 else pltpu.roll(x, shift, 1)


def dot(a, b, dims, precision=None):
    return lax.dot_general(a, b, (dims, ((), ())), precision=precision, preferred_element_type=F32)


def table_kernel(scale_ref, embed_ref, time_ref, w1_ref, w2_ref, w3_ref, tab_ref, f_ref, h1_ref, h2_ref, raw):
    scale = scale_ref[...].astype(F32) * (1.0 / 64.0)
    feature = (embed_ref[...].astype(F32) + scale * time_ref[...].astype(F32)).astype(BF16)
    one = jnp.tanh(dot(feature, w1_ref[...], ((1,), (0,)))).astype(BF16)
    two = jnp.tanh(dot(one, w2_ref[...], ((1,), (0,)))).astype(BF16)
    f_ref[...] = feature.astype(F32)
    h1_ref[...] = one.astype(F32)
    h2_ref[...] = two.astype(F32)
    logits = dot(w3_ref[...], two, ((0,), (1,)))
    raw[...] = jnp.zeros_like(raw)
    tab_ref[...] = jnp.zeros_like(tab_ref)
    for a in range(ACTIONS):
        raw[8 * a : 8 * a + POINTS, 0:CLASSES] = logits[a * POINTS : (a + 1) * POINTS]
    valid = lax.broadcasted_iota(jnp.int32, (8, COLS), 0) < POINTS
    for a in range(ACTIONS):
        x = raw[8 * a : 8 * a + 8, :]
        weight = jnp.maximum(x, 0.0) + jnp.log(1.0 + jnp.exp(-jnp.abs(x))) + SLACK
        total = jnp.sum(jnp.where(valid, weight, 0.0), axis=0, keepdims=True)
        tab_ref[16 * a : 16 * a + 8, :] = DECAY * weight / total
        tab_ref[16 * a + 8 : 16 * a + 16, :] = 1.0 / ((1.0 + jnp.exp(-x)) * total)
    tab_ref[64:68, 0:CLASSES] = logits[ACTIONS * POINTS :]


def chance_row(a, k):
    return 16 * a + k


def slope_row(a, k):
    return 16 * a + 8 + k


def bonus_row(a):
    return 64 + a


def class_plane(buf_ref, own_ref):
    up, down = buf_ref
    return up, own_ref[...].astype(F32) + 1.0, down


def fill_rows(dst, g, up, mid, down, n):
    dst[g, TOP - n : TOP, :] = up
    dst[g, TOP : TOP + ROWS, :] = mid
    dst[g, TOP + ROWS : TOP + ROWS + n, :] = down


def extend_rows(v_ref, r_ref, s_ref, c_ref, up_ref, down_ref, val, rew, sen, cls):
    def one(g, carry):
        up = up_ref[g].astype(F32)
        down = down_ref[g].astype(F32)
        fill_rows(val, g, up[0:6], v_ref[g].astype(F32), down[0:6], VH)
        fill_rows(rew, g, up[6:11], r_ref[g].astype(F32), down[6:11], RH)
        fill_rows(sen, g, up[11:14], s_ref[g].astype(F32), down[11:14], FH)
        return carry

    lax.fori_loop(0, GOALS, one, 0, unroll=4)
    cls[...] = jnp.zeros_like(cls)
    cls[TOP : TOP + ROWS, :] = c_ref[...].astype(F32) + 1.0
    for i in range(RH):
        cls[TOP - RH + i : TOP - RH + i + 1, :] = up_ref[i, 14:15, :].astype(F32)
        cls[TOP + ROWS + i : TOP + ROWS + i + 1, :] = down_ref[i, 14:15, :].astype(F32)


def strip_kernel(v_ref, r_ref, s_ref, c_ref, up_ref, down_ref, to_right, to_left, val, rew, sen, cls):
    extend_rows(v_ref, r_ref, s_ref, c_ref, up_ref, down_ref, val, rew, sen, cls)
    group_lane = lane_iota((8, COLS)) % GROUP
    group_at = lane_iota((8, COLS)) // GROUP

    def tile(i, carry):
        o, j = i // 4, i % 4
        rows = pl.ds(pl.multiple_of(8 + 8 * j, 8), 8)
        right = jnp.zeros((8, COLS), F32)
        left = jnp.zeros((8, COLS), F32)
        for q in range(8):
            p = GROUP * q
            v, r, s = val[o * 8 + q, rows, :], rew[o * 8 + q, rows, :], sen[o * 8 + q, rows, :]
            here = group_at == q
            part = jnp.where(group_lane < 6, turn(v, p + 6), jnp.where(group_lane < 11, turn(r, p + 11), turn(s, p + 14)))
            right = jnp.where(here, part, right)
            part = jnp.where(group_lane < 6, turn(v, p), jnp.where(group_lane < 11, turn(r, p + 6), turn(s, p + 11)))
            left = jnp.where(here, part, left)
        to_right[o, pl.ds(pl.multiple_of(8 * j, 8), 8), :] = right
        to_left[o, pl.ds(pl.multiple_of(8 * j, 8), 8), :] = left
        return carry

    lax.fori_loop(0, OCT * 4, tile, 0)
    for j in range(4):
        c = cls[8 + 8 * j : 16 + 8 * j, :]
        right = jnp.zeros((8, COLS), F32)
        left = jnp.zeros((8, COLS), F32)
        for q in range(8):
            here = group_at == q
            right = jnp.where(here, turn(c, GROUP * q + 6), right)
            left = jnp.where(here, turn(c, GROUP * q), left)
        to_right[OCT, 8 * j : 8 * j + 8, :] = right
        to_left[OCT, 8 * j : 8 * j + 8, :] = left


def main_kernel(v_ref, r_ref, s_ref, c_ref, up_ref, down_ref, lb_ref, rb_ref, tab_ref,
                snap_ref, pay_ref, sums_ref,
                val, rew, sen, cls, sval, srew, ssen, scls,
                chance, schance, bonus, sbonus, mask, smask, slope,
                soft, ssoft, lshift, rshift, push, spush, cgrad, paysum, packed):
    extend_rows(v_ref, r_ref, s_ref, c_ref, up_ref, down_ref, val.at[0], rew, sen, cls)
    lane = lane_iota((8, COLS))
    glane = lane % GROUP
    inner = glane < 6
    first, last = lane == 0, lane == COLS - 1
    strip_first, strip_last = glane == 5, glane == 6
    for o in range(OCT + 1):
        for j in range(4):
            left = lb_ref[o, 8 * j : 8 * j + 8, :].astype(F32)
            right = rb_ref[o, 8 * j : 8 * j + 8, :].astype(F32)
            at = slice(8 + 8 * j, 16 + 8 * j)
            outer = jnp.where(inner, left, turn(right, 6))
            if o == OCT:
                scls[at, :] = jnp.where(glane < 12, outer, 0.0)
            else:
                sval[0, o, at, :] = outer
                srew[o, at, :] = jnp.where(inner, turn(left, -5), right)
                ssen[o, at, :] = jnp.where(inner, turn(left, -8), turn(right, -5))
    for j in range(4):
        at = slice(8 + 8 * j, 16 + 8 * j)
        for source, ch, bo, ma in ((cls, chance, bonus, mask), (scls, schance, sbonus, smask)):
            number = source[at, :].astype(jnp.int32)
            inside = number > 0
            which = jnp.maximum(number - 1, 0)
            ma[at, :] = inside.astype(F32)

            def look(row):
                table = jnp.broadcast_to(tab_ref[row : row + 1, :], (8, COLS))
                return jnp.where(inside, jnp.take_along_axis(table, which, axis=1), 0.0)

            for a in range(ACTIONS):
                for k in range(POINTS):
                    ch[a * POINTS + k, at, :] = look(chance_row(a, k))
                    if source is cls and j in (1, 2):
                        slope[a * POINTS + k, 8 * j - 8 : 8 * j, :] = look(slope_row(a, k))
                bo[a, at, :] = look(bonus_row(a))

    def where_tile(j):
        base = pl.multiple_of(8 + 8 * j, 8)
        return pl.ds(base, 8), pl.ds(base - 1, 8), pl.ds(base + 1, 8)

    def soft_step(near, reward, ch, bo, keep_value):
        q = []
        for a in range(ACTIONS):
            total = reward + bo[a]
            for k in range(POINTS):
                total = total + ch[a * POINTS + k] * near[k]
            q.append(total)
        highest = jnp.maximum(jnp.maximum(q[0], q[1]), jnp.maximum(q[2], q[3]))
        e = [jnp.exp(x - highest) for x in q]
        total = (e[0] + e[1]) + (e[2] + e[3])
        inverse = 1.0 / total
        value = highest + jnp.log(total) if keep_value else None
        return [x * inverse for x in e], value

    for t in range(ITERS):
        keep = t < ITERS - 1

        def forward(i, carry, t=t, keep=keep):
            o, j = i // 4, i % 4
            rows, above, below = where_tile(j)
            ch = [chance[n, rows, :] for n in range(ACTIONS * POINTS)]
            bo = [bonus[a, rows, :] for a in range(ACTIONS)]
            sv = sval[t, o, rows, :]
            edge = jnp.zeros((8, COLS), F32)
            for q in range(8):
                p, g = GROUP * q, o * 8 + q
                x = val[t, g, rows, :]
                fill = turn(sv, -(p + 6))
                toleft = turn(jnp.where(last, fill, x), 1)
                toright = turn(jnp.where(first, fill, x), -1)
                edge = jnp.where((lane == p + 5) | (lane == p + 6), turn(x, p + 6), edge)
                lshift[t, g, rows, :] = toleft
                rshift[t, g, rows, :] = toright
                near = [x, val[t, g, above, :], val[t, g, below, :], toleft, toright]
                probs, value = soft_step(near, rew[g, rows, :], ch, bo, keep)
                for a in range(ACTIONS):
                    soft[t, a, g, rows, :] = probs[a]
                if keep:
                    val[t + 1, g, rows, :] = value * mask[rows, :]
            near = [sv, sval[t, o, above, :], sval[t, o, below, :],
                    turn(jnp.where(strip_first, edge, sv), 1), turn(jnp.where(strip_last, edge, sv), -1)]
            ch = [schance[n, rows, :] for n in range(ACTIONS * POINTS)]
            bo = [sbonus[a, rows, :] for a in range(ACTIONS)]
            probs, value = soft_step(near, srew[o, rows, :], ch, bo, keep)
            for a in range(ACTIONS):
                ssoft[t, a, o, rows, :] = probs[a]
            if keep:
                sval[t + 1, o, rows, :] = value * smask[rows, :]
            return carry

        lax.fori_loop(0, OCT * 4, forward, 0)

    cgrad[...] = jnp.zeros_like(cgrad)
    paysum[...] = jnp.zeros_like(paysum)

    def gather(o, rows, above, below, old):
        s3, s4 = spush[old, 3, o, rows, :], spush[old, 4, o, rows, :]
        both = jnp.where(strip_last, s3, s4)
        edge = jnp.zeros((8, COLS), F32)
        out = []
        for q in range(8):
            p, g = GROUP * q, o * 8 + q
            p3, p4 = push[old, 3, g, rows, :], push[old, 4, g, rows, :]
            fill = turn(both, -(p + 6))
            from_right = turn(jnp.where(first, fill, p3), -1)
            from_left = turn(jnp.where(last, fill, p4), 1)
            edge = jnp.where((lane == p + 5) | (lane == p + 6), turn(jnp.where(first, p3, p4), p + 6), edge)
            out.append(push[old, 0, g, rows, :] + push[old, 1, g, below, :] + push[old, 2, g, above, :]
                       + from_right + from_left)
        strip = (spush[old, 0, o, rows, :] + spush[old, 1, o, below, :] + spush[old, 2, o, above, :]
                 + turn(jnp.where(strip_last, edge, s3), -1) + turn(jnp.where(strip_first, edge, s4), 1))
        return out, strip

    for t in reversed(range(ITERS)):
        new, old = t % 2, (t + 1) % 2

        def backward(o, j, own, t=t, new=new, old=old):
            rows, above, below = where_tile(j)
            if t == ITERS - 1:
                adj = [sen[o * 8 + q, rows, :] for q in range(8)]
                strip = ssen[o, rows, :]
            else:
                adj, strip = gather(o, rows, above, below, old)
            for q in range(8):
                g = o * 8 + q
                grads = [adj[q] * soft[t, a, g, rows, :] for a in range(ACTIONS)]
                for k in range(POINTS):
                    total = grads[0] * chance[k, rows, :]
                    for a in range(1, ACTIONS):
                        total = total + grads[a] * chance[a * POINTS + k, rows, :]
                    push[new, k, g, rows, :] = total
                if own:
                    at = pl.ds(pl.multiple_of(8 * j - 8, 8), 8)
                    paysum[g, at, :] += (grads[0] + grads[1]) + (grads[2] + grads[3])
                    near = [val[t, g, rows, :], val[t, g, above, :], val[t, g, below, :],
                            lshift[t, g, rows, :], rshift[t, g, rows, :]]
                    for a in range(ACTIONS):
                        for k in range(POINTS):
                            cgrad[a * POINTS + k, at, :] += grads[a] * near[k]
                        cgrad[ACTIONS * POINTS + a, at, :] += grads[a]
            grads = [strip * ssoft[t, a, o, rows, :] for a in range(ACTIONS)]
            for k in range(POINTS):
                total = grads[0] * schance[k, rows, :]
                for a in range(1, ACTIONS):
                    total = total + grads[a] * schance[a * POINTS + k, rows, :]
                spush[new, k, o, rows, :] = total

        def outer_rows(i, carry):
            backward(i // 2, 3 * (i % 2), False)
            return carry

        def own_rows(i, carry):
            backward(i // 2, 1 + i % 2, True)
            return carry

        lax.fori_loop(0, OCT * 2, outer_rows, 0)
        lax.fori_loop(0, OCT * 2, own_rows, 0)

    def finish(i, carry):
        o, j = i // 2, 1 + i % 2
        rows, above, below = where_tile(j)
        adj = gather(o, rows, above, below, 0)[0]
        at = pl.ds(pl.multiple_of(8 * j - 8, 8), 8)
        for q in range(8):
            packed[o * 8 + q, at, :] = adj[q]
        return carry

    lax.fori_loop(0, OCT * 2, finish, 0)
    snap_ref[...] = packed[...].astype(BF16)
    pay_ref[...] = paysum[...].astype(BF16)
    for j in range(2):
        at = slice(8 * j, 8 * j + 8)
        rows = slice(TOP + 8 * j, TOP + 8 * j + 8)
        for a in range(ACTIONS):
            grads = [cgrad[a * POINTS + k, at, :] for k in range(POINTS)]
            weighted = grads[0] * chance[a * POINTS, rows, :]
            for k in range(1, POINTS):
                weighted = weighted + grads[k] * chance[a * POINTS + k, rows, :]
            for k in range(POINTS):
                cgrad[a * POINTS + k, at, :] = (DECAY * grads[k] - weighted) * slope[a * POINTS + k, at, :]
    number = lax.broadcasted_iota(jnp.int32, (CLASSES, COLS), 0)
    total = jnp.zeros((CLASSES, OUTS), F32)
    for i in range(ROWS):
        one_hot = (number == c_ref[i : i + 1, :]).astype(BF16)
        total = total + dot(one_hot, cgrad[:, i, :].astype(BF16), ((1,), (1,)))
    packed[0, :, :] = jnp.zeros((ROWS, COLS), F32)
    packed[0, 0:CLASSES, 0:OUTS] = total
    sums_ref[...] = packed[0, 0:8, :] + turn(packed[0, 8:16, :], 32)


def last_kernel(parts_ref, scale_ref, f_ref, h1_ref, h2_ref, w1_ref, w2_ref, w3_ref,
                embed_ref, time_ref, one_ref, two_ref, three_ref, *, factor):
    total = parts_ref[0]
    for i in range(1, parts_ref.shape[0]):
        total = total + parts_ref[i]
    total = total * factor
    sums = jnp.concatenate([total[:, 0:OUTS], turn(total, -32)[:, 0:OUTS]], axis=0)
    f, h1, h2 = f_ref[...], h1_ref[...], h2_ref[...]
    two_grad = dot(sums, w3_ref[...].astype(F32), ((1,), (1,)), HIGHEST) * (1.0 - h2 * h2)
    one_grad = dot(two_grad, w2_ref[...].astype(F32), ((1,), (1,)), HIGHEST) * (1.0 - h1 * h1)
    feature_grad = dot(one_grad, w1_ref[...].astype(F32), ((1,), (1,)), HIGHEST)
    three_ref[...] = dot(h2, sums, ((0,), (0,)), HIGHEST)
    two_ref[...] = dot(h1, two_grad, ((0,), (0,)), HIGHEST)
    one_ref[...] = dot(f, one_grad, ((0,), (0,)), HIGHEST)
    embed_ref[...] = feature_grad
    scale = scale_ref[...].astype(F32) * (1.0 / 64.0)
    time_ref[...] = scale * jnp.sum(feature_grad, axis=0, keepdims=True)


def shift(x, axis, step):
    size = lax.axis_size(axis)
    pairs = [(i, i + step) for i in range(size) if 0 <= i + step < size]
    return lax.ppermute(x, axis, pairs)


def spread(x, axis):
    size = lax.axis_size(axis)
    return lax.all_to_all(jnp.broadcast_to(x[None], (size,) + x.shape), axis, 0, 0, tiled=True)


def body(classes, check_index, snapshot, payoff, sensitivity, embed, time_vec, w_one, w_two, w_three):
    sd = jax.ShapeDtypeStruct
    marked = (classes + 1).astype(BF16)

    def edge_rows(v, r, s, c):
        c = jnp.pad(c[:, None, :], ((0, GOALS - RH), (0, 1), (0, 0)))
        return jnp.concatenate([v, r, s, c], axis=1)

    to_down = edge_rows(snapshot[:, -VH:], payoff[:, -RH:], sensitivity[:, -FH:], marked[-RH:])
    to_up = edge_rows(snapshot[:, :VH], payoff[:, :RH], sensitivity[:, :FH], marked[:RH])
    up = shift(to_down, "row", 1)
    down = shift(to_up, "row", -1)

    scale = jnp.broadcast_to(check_index.reshape(1, 1), (1, 64))
    layer = sd((CLASSES, 64), F32)
    table, feature, one, two = vmem_call(
        table_kernel, (sd((72, COLS), F32), layer, layer, layer), [pltpu.VMEM((32, COLS), F32)]
    )(scale, embed, time_vec.reshape(1, -1), w_one, w_two, w_three)

    ext = pltpu.VMEM((GOALS, EXT, COLS), F32)
    plane = pltpu.VMEM((EXT, COLS), F32)
    edge = sd((OCT + 1, 32, COLS), F32)
    to_right, to_left = vmem_call(strip_kernel, (edge, edge), [ext, ext, ext, plane])(
        snapshot, payoff, sensitivity, classes, up, down
    )
    left = shift(to_right.astype(BF16), "col", 1)
    right = shift(to_left.astype(BF16), "col", -1)

    tile = sd((GOALS, ROWS, COLS), BF16)
    strip = pltpu.VMEM((OCT, EXT, COLS), F32)

    def many(*shape):
        return pltpu.VMEM(shape + (COLS,), F32)

    n = ACTIONS * POINTS
    snap, pay, sums = vmem_call(
        main_kernel,
        (tile, tile, sd((8, COLS), F32)),
        [
            many(ITERS, GOALS, EXT), ext, ext, plane,
            many(ITERS, OCT, EXT), strip, strip, plane,
            many(n, EXT), many(n, EXT), many(ACTIONS, EXT), many(ACTIONS, EXT), plane, plane, many(n, ROWS),
            many(ITERS, ACTIONS, GOALS, EXT), many(ITERS, ACTIONS, OCT, EXT),
            many(ITERS, GOALS, EXT), many(ITERS, GOALS, EXT),
            many(2, POINTS, GOALS, EXT), many(2, POINTS, OCT, EXT),
            many(OUTS, ROWS), many(GOALS, ROWS), many(GOALS, ROWS),
        ],
    )(snapshot, payoff, sensitivity, classes, up, down, left, right, table)

    sums = jnp.sum(spread(sums, "row"), axis=0)
    parts = spread(sums, "col")
    factor = 1.0 / math.sqrt(ROWS * lax.axis_size("row") * COLS * lax.axis_size("col"))

    def last(*refs):
        last_kernel(*refs, factor=factor)

    grads = vmem_call(
        last, (layer, sd((1, 64), F32), sd((64, 64), F32), sd((64, 64), F32), sd((64, OUTS), F32))
    )(parts, scale, feature, one, two, w_one, w_two, w_three)
    return (snap, pay, grads[0], grads[1].reshape(64), grads[2], grads[3], grads[4])


def solution(mesh):
    tiled = P(None, "row", "col")
    return jax.shard_map(
        body,
        mesh=mesh,
        in_specs=(P("row", "col"), P(), tiled, tiled, tiled, P(), P(), P(), P(), P()),
        out_specs=(tiled, tiled, P(), P(), P(), P(), P()),
        check_vma=False,
    )
```

```python
import math

import jax
import jax.numpy as jnp
from jax import lax
from jax.experimental import pallas as pl
from jax.experimental.pallas import tpu as pltpu
from jax.sharding import PartitionSpec as P

ITERS = 3
ACTIONS = 4
POINTS = 5
OUTS = 24
GOALS = 24
CLASSES = 16
ROWS = 16
COLS = 128
DECAY = 0.9
SLACK = 0.05
VH, RH, FH = 6, 5, 3
TOP = 16
EXT = 48
GROUP = 16
OCT = GOALS // 8
HIGHEST = lax.Precision.HIGHEST
F32 = jnp.float32
BF16 = jnp.bfloat16


def vmem_call(kernel, out_shape, scratch=(), limit=48 * 1024 * 1024, source=pltpu.VMEM):
    whole = pl.BlockSpec(memory_space=pltpu.VMEM)
    given = pl.BlockSpec(memory_space=source)
    return lambda *args: pl.pallas_call(
        kernel,
        out_shape=out_shape,
        in_specs=[given] * len(args),
        out_specs=jax.tree.map(lambda _: whole, out_shape),
        scratch_shapes=list(scratch),
        compiler_params=pltpu.CompilerParams(vmem_limit_bytes=limit),
    )(*args)


def lane_iota(shape):
    return lax.broadcasted_iota(jnp.int32, shape, len(shape) - 1)


def turn(x, shift):
    shift = shift % COLS
    return x if shift == 0 else pltpu.roll(x, shift, 1)


def dot(a, b, dims, precision=None):
    return lax.dot_general(a, b, (dims, ((), ())), precision=precision, preferred_element_type=F32)


def table_kernel(scale_ref, embed_ref, time_ref, w1_ref, w2_ref, w3_ref, tab_ref, f_ref, h1_ref, h2_ref, raw):
    scale = scale_ref[...].astype(F32) * (1.0 / 64.0)
    feature = (embed_ref[...].astype(F32) + scale * time_ref[...].astype(F32)).astype(BF16)
    one = jnp.tanh(dot(feature, w1_ref[...], ((1,), (0,)))).astype(BF16)
    two = jnp.tanh(dot(one, w2_ref[...], ((1,), (0,)))).astype(BF16)
    f_ref[...] = feature.astype(F32)
    h1_ref[...] = one.astype(F32)
    h2_ref[...] = two.astype(F32)
    logits = dot(w3_ref[...], two, ((1,), (1,)))
    raw[...] = jnp.zeros_like(raw)
    tab_ref[...] = jnp.zeros_like(tab_ref)
    for a in range(ACTIONS):
        raw[8 * a : 8 * a + POINTS, 0:CLASSES] = logits[a * POINTS : (a + 1) * POINTS]
    valid = lax.broadcasted_iota(jnp.int32, (8, COLS), 0) < POINTS
    for a in range(ACTIONS):
        x = raw[8 * a : 8 * a + 8, :]
        weight = jnp.maximum(x, 0.0) + jnp.log(1.0 + jnp.exp(-jnp.abs(x))) + SLACK
        total = jnp.sum(jnp.where(valid, weight, 0.0), axis=0, keepdims=True)
        tab_ref[16 * a : 16 * a + 8, :] = DECAY * weight / total
        tab_ref[16 * a + 8 : 16 * a + 16, :] = 1.0 / ((1.0 + jnp.exp(-x)) * total)
    tab_ref[64:68, 0:CLASSES] = logits[ACTIONS * POINTS :]


def chance_row(a, k):
    return 16 * a + k


def slope_row(a, k):
    return 16 * a + 8 + k


def bonus_row(a):
    return 64 + a


def edge_kernel(v_hbm, r_hbm, s_hbm, c_hbm, to_down, to_up, low, high, v_ref, r_ref, s_ref, c_ref, sems):
    pairs = ((v_hbm, v_ref), (r_hbm, r_ref), (s_hbm, s_ref), (c_hbm, c_ref))
    copies = [pltpu.make_async_copy(a, b, sems.at[i]) for i, (a, b) in enumerate(pairs)]
    for copy in copies:
        copy.start()
    for copy in copies:
        copy.wait()
    low[...] = jnp.zeros_like(low)
    high[...] = jnp.zeros_like(high)
    marked = c_ref[...].astype(F32) + 1.0
    for g in range(GOALS):
        v, r, s = v_ref[g].astype(F32), r_ref[g].astype(F32), s_ref[g].astype(F32)
        low[0:6, :], low[6:11, :], low[11:14, :] = v[ROWS - VH :], r[ROWS - RH :], s[ROWS - FH :]
        high[0:6, :], high[6:11, :], high[11:14, :] = v[0:VH], r[0:RH], s[0:FH]
        if g < RH:
            low[14:15, :], high[14:15, :] = marked[ROWS - RH + g : ROWS - RH + g + 1], marked[g : g + 1]
        to_down[g] = low[...].astype(BF16)
        to_up[g] = high[...].astype(BF16)


def fill_rows(dst, g, up, mid, down, n):
    dst[g, TOP - n : TOP, :] = up
    dst[g, TOP : TOP + ROWS, :] = mid
    dst[g, TOP + ROWS : TOP + ROWS + n, :] = down


def extend_rows(v_ref, r_ref, s_ref, c_ref, up_ref, down_ref, val, rew, sen, cls):
    def one(g, carry):
        up = up_ref[g].astype(F32)
        down = down_ref[g].astype(F32)
        fill_rows(val, g, up[0:6], v_ref[g].astype(F32), down[0:6], VH)
        fill_rows(rew, g, up[6:11], r_ref[g].astype(F32), down[6:11], RH)
        fill_rows(sen, g, up[11:14], s_ref[g].astype(F32), down[11:14], FH)
        return carry

    lax.fori_loop(0, GOALS, one, 0, unroll=4)
    cls[...] = jnp.zeros_like(cls)
    cls[TOP : TOP + ROWS, :] = c_ref[...].astype(F32) + 1.0
    for i in range(RH):
        cls[TOP - RH + i : TOP - RH + i + 1, :] = up_ref[i, 14:15, :].astype(F32)
        cls[TOP + ROWS + i : TOP + ROWS + i + 1, :] = down_ref[i, 14:15, :].astype(F32)


def strip_kernel(v_ref, r_ref, s_ref, c_ref, up_ref, down_ref, to_right, to_left, val, rew, sen, cls):
    extend_rows(v_ref, r_ref, s_ref, c_ref, up_ref, down_ref, val, rew, sen, cls)
    group_lane = lane_iota((8, COLS)) % GROUP
    group_at = lane_iota((8, COLS)) // GROUP

    def octet(o, carry):
        for j in range(4):
            rows = slice(8 + 8 * j, 16 + 8 * j)
            right = jnp.zeros((8, COLS), F32)
            left = jnp.zeros((8, COLS), F32)
            for q in range(8):
                p = GROUP * q
                v, r, s = val[o * 8 + q, rows, :], rew[o * 8 + q, rows, :], sen[o * 8 + q, rows, :]
                here = group_at == q
                part = jnp.where(group_lane < 11, turn(r, p + 11), turn(s, p + 14))
                right = jnp.where(here, jnp.where(group_lane < 6, turn(v, p + 6), part), right)
                part = jnp.where(group_lane < 11, turn(r, p + 6), turn(s, p + 11))
                left = jnp.where(here, jnp.where(group_lane < 6, turn(v, p), part), left)
            to_right[o, 8 * j : 8 * j + 8, :] = right.astype(to_right.dtype)
            to_left[o, 8 * j : 8 * j + 8, :] = left.astype(to_left.dtype)
        return carry

    lax.fori_loop(0, OCT, octet, 0)
    for j in range(4):
        c = cls[8 + 8 * j : 16 + 8 * j, :]
        right = jnp.zeros((8, COLS), F32)
        left = jnp.zeros((8, COLS), F32)
        for q in range(8):
            here = group_at == q
            right = jnp.where(here, turn(c, GROUP * q + 6), right)
            left = jnp.where(here, turn(c, GROUP * q), left)
        to_right[OCT, 8 * j : 8 * j + 8, :] = right.astype(to_right.dtype)
        to_left[OCT, 8 * j : 8 * j + 8, :] = left.astype(to_left.dtype)


def main_kernel(v_ref, r_ref, s_ref, c_ref, up_ref, down_ref, lb_ref, rb_ref, tab_ref,
                snap_ref, pay_ref, sums_ref,
                val, rew, sen, cls, sval, srew, ssen, scls,
                chance, schance, bonus, sbonus, mask, smask, slope,
                soft, ssoft, lshift, rshift, push, spush, cgrad, paysum, packed):
    extend_rows(v_ref, r_ref, s_ref, c_ref, up_ref, down_ref, val.at[0], rew, sen, cls)
    lane = lane_iota((8, COLS))
    glane = lane % GROUP
    inner = glane < 6
    first, last = lane == 0, lane == COLS - 1
    strip_first, strip_last = glane == 5, glane == 6
    for o in range(OCT + 1):
        for j in range(4):
            left = lb_ref[o, 8 * j : 8 * j + 8, :].astype(F32)
            right = rb_ref[o, 8 * j : 8 * j + 8, :].astype(F32)
            at = slice(8 + 8 * j, 16 + 8 * j)
            outer = jnp.where(inner, left, turn(right, 6))
            if o == OCT:
                scls[at, :] = jnp.where(glane < 12, outer, 0.0)
            else:
                sval[0, o, at, :] = outer
                srew[o, at, :] = jnp.where(inner, turn(left, -5), right)
                ssen[o, at, :] = jnp.where(inner, turn(left, -8), turn(right, -5))
    for j in range(4):
        at = slice(8 + 8 * j, 16 + 8 * j)
        for source, ch, bo, ma in ((cls, chance, bonus, mask), (scls, schance, sbonus, smask)):
            number = source[at, :].astype(jnp.int32)
            inside = number > 0
            which = jnp.maximum(number - 1, 0)
            ma[at, :] = inside.astype(F32)

            def look(row):
                table = jnp.broadcast_to(tab_ref[row : row + 1, :], (8, COLS))
                return jnp.where(inside, jnp.take_along_axis(table, which, axis=1), 0.0)

            for a in range(ACTIONS):
                for k in range(POINTS):
                    ch[a * POINTS + k, at, :] = look(chance_row(a, k))
                    if source is cls and j in (1, 2):
                        slope[a * POINTS + k, 8 * j - 8 : 8 * j, :] = look(slope_row(a, k))
                bo[a, at, :] = look(bonus_row(a))

    def where_tile(j):
        base = 8 + 8 * j
        return slice(base, base + 8), slice(base - 1, base + 7), slice(base + 1, base + 9)

    def soft_step(near, reward, ch, bo, keep_value):
        q = []
        for a in range(ACTIONS):
            total = reward + bo[a]
            for k in range(POINTS):
                total = total + ch[a * POINTS + k] * near[k]
            q.append(total)
        highest = jnp.maximum(jnp.maximum(q[0], q[1]), jnp.maximum(q[2], q[3]))
        e = [jnp.exp(x - highest) for x in q]
        total = (e[0] + e[1]) + (e[2] + e[3])
        inverse = 1.0 / total
        value = highest + jnp.log(total) if keep_value else None
        return [x * inverse for x in e], value

    for t in range(ITERS):
        keep = t < ITERS - 1

        def forward(o, j, t=t, keep=keep):
            rows, above, below = where_tile(j)
            ch = [chance[n, rows, :] for n in range(ACTIONS * POINTS)]
            bo = [bonus[a, rows, :] for a in range(ACTIONS)]
            sv = sval[t, o, rows, :]
            edge = jnp.zeros((8, COLS), F32)
            for q in range(8):
                p, g = GROUP * q, o * 8 + q
                x = val[t, g, rows, :]
                fill = turn(sv, -(p + 6))
                toleft = turn(jnp.where(last, fill, x), 1)
                toright = turn(jnp.where(first, fill, x), -1)
                edge = jnp.where((lane == p + 5) | (lane == p + 6), turn(x, p + 6), edge)
                lshift[t, g, rows, :] = toleft
                rshift[t, g, rows, :] = toright
                near = [x, val[t, g, above, :], val[t, g, below, :], toleft, toright]
                probs, value = soft_step(near, rew[g, rows, :], ch, bo, keep)
                for a in range(ACTIONS):
                    soft[t, a, g, rows, :] = probs[a]
                if keep:
                    val[t + 1, g, rows, :] = value * mask[rows, :]
            near = [sv, sval[t, o, above, :], sval[t, o, below, :],
                    turn(jnp.where(strip_first, edge, sv), 1), turn(jnp.where(strip_last, edge, sv), -1)]
            ch = [schance[n, rows, :] for n in range(ACTIONS * POINTS)]
            bo = [sbonus[a, rows, :] for a in range(ACTIONS)]
            probs, value = soft_step(near, srew[o, rows, :], ch, bo, keep)
            for a in range(ACTIONS):
                ssoft[t, a, o, rows, :] = probs[a]
            if keep:
                sval[t + 1, o, rows, :] = value * smask[rows, :]

        def forward_all(o, carry, forward=forward):
            for j in range(4):
                forward(o, j)
            return carry

        lax.fori_loop(0, OCT, forward_all, 0)

    cgrad[...] = jnp.zeros_like(cgrad)
    paysum[...] = jnp.zeros_like(paysum)

    def gather(o, rows, above, below, old):
        s3, s4 = spush[old, 3, o, rows, :], spush[old, 4, o, rows, :]
        both = jnp.where(strip_last, s3, s4)
        edge = jnp.zeros((8, COLS), F32)
        out = []
        for q in range(8):
            p, g = GROUP * q, o * 8 + q
            p3, p4 = push[old, 3, g, rows, :], push[old, 4, g, rows, :]
            fill = turn(both, -(p + 6))
            from_right = turn(jnp.where(first, fill, p3), -1)
            from_left = turn(jnp.where(last, fill, p4), 1)
            edge = jnp.where((lane == p + 5) | (lane == p + 6), turn(jnp.where(first, p3, p4), p + 6), edge)
            out.append(push[old, 0, g, rows, :] + push[old, 1, g, below, :] + push[old, 2, g, above, :]
                       + from_right + from_left)
        strip = (spush[old, 0, o, rows, :] + spush[old, 1, o, below, :] + spush[old, 2, o, above, :]
                 + turn(jnp.where(strip_last, edge, s3), -1) + turn(jnp.where(strip_first, edge, s4), 1))
        return out, strip

    for t in reversed(range(ITERS)):
        new, old = t % 2, (t + 1) % 2

        def backward(o, j, own, t=t, new=new, old=old):
            rows, above, below = where_tile(j)
            if t == ITERS - 1:
                adj = [sen[o * 8 + q, rows, :] for q in range(8)]
                strip = ssen[o, rows, :]
            else:
                adj, strip = gather(o, rows, above, below, old)
            for q in range(8):
                g = o * 8 + q
                grads = [adj[q] * soft[t, a, g, rows, :] for a in range(ACTIONS)]
                for k in range(POINTS):
                    total = grads[0] * chance[k, rows, :]
                    for a in range(1, ACTIONS):
                        total = total + grads[a] * chance[a * POINTS + k, rows, :]
                    push[new, k, g, rows, :] = total
            if own:
                at = slice(8 * j - 8, 8 * j)
                for q in range(8):
                    g = o * 8 + q
                    grads = [adj[q] * soft[t, a, g, rows, :] for a in range(ACTIONS)]
                    paysum[g, at, :] += (grads[0] + grads[1]) + (grads[2] + grads[3])
                for a in range(ACTIONS):
                    sums = [cgrad[a * POINTS + k, at, :] for k in range(POINTS)]
                    total = cgrad[ACTIONS * POINTS + a, at, :]
                    for q in range(8):
                        g = o * 8 + q
                        grad = adj[q] * soft[t, a, g, rows, :]
                        total = total + grad
                        near = [val[t, g, rows, :], val[t, g, above, :], val[t, g, below, :],
                                lshift[t, g, rows, :], rshift[t, g, rows, :]]
                        sums = [x + grad * y for x, y in zip(sums, near)]
                    for k in range(POINTS):
                        cgrad[a * POINTS + k, at, :] = sums[k]
                    cgrad[ACTIONS * POINTS + a, at, :] = total
            grads = [strip * ssoft[t, a, o, rows, :] for a in range(ACTIONS)]
            for k in range(POINTS):
                total = grads[0] * schance[k, rows, :]
                for a in range(1, ACTIONS):
                    total = total + grads[a] * schance[a * POINTS + k, rows, :]
                spush[new, k, o, rows, :] = total

        def backward_all(o, carry, backward=backward):
            for j in range(4):
                backward(o, j, j in (1, 2))
            return carry

        lax.fori_loop(0, OCT, backward_all, 0)

    def finish(o, carry):
        for j in (1, 2):
            rows, above, below = where_tile(j)
            adj = gather(o, rows, above, below, 0)[0]
            for q in range(8):
                packed[o * 8 + q, 8 * j - 8 : 8 * j, :] = adj[q]
        return carry

    lax.fori_loop(0, OCT, finish, 0)
    snap_ref[...] = packed[...].astype(BF16)
    pay_ref[...] = paysum[...].astype(BF16)
    for j in range(2):
        at = slice(8 * j, 8 * j + 8)
        rows = slice(TOP + 8 * j, TOP + 8 * j + 8)
        for a in range(ACTIONS):
            grads = [cgrad[a * POINTS + k, at, :] for k in range(POINTS)]
            weighted = grads[0] * chance[a * POINTS, rows, :]
            for k in range(1, POINTS):
                weighted = weighted + grads[k] * chance[a * POINTS + k, rows, :]
            for k in range(POINTS):
                cgrad[a * POINTS + k, at, :] = (DECAY * grads[k] - weighted) * slope[a * POINTS + k, at, :]
    number = lax.broadcasted_iota(jnp.int32, (CLASSES, COLS), 0)
    total = jnp.zeros((CLASSES, OUTS), F32)
    for i in range(ROWS):
        one_hot = (number == c_ref[i : i + 1, :]).astype(BF16)
        total = total + dot(one_hot, cgrad[:, i, :].astype(BF16), ((1,), (1,)))
    packed[0, :, :] = jnp.zeros((ROWS, COLS), F32)
    packed[0, 0:CLASSES, 0:OUTS] = total
    parts = [packed[0, 4 * q : 4 * q + 4, :] for q in range(4)]
    sums_ref[...] = (parts[0] + turn(parts[1], 32)) + (turn(parts[2], 64) + turn(parts[3], 96))


def last_kernel(parts_ref, scale_ref, f_ref, h1_ref, h2_ref, w1_ref, w2_ref, w3_ref,
                embed_ref, time_ref, one_ref, two_ref, three_ref, classed, *, factor):
    total = parts_ref[0]
    for i in range(1, parts_ref.shape[0]):
        total = total + parts_ref[i]
    total = total * factor
    for q in range(4):
        classed[4 * q : 4 * q + 4, :] = turn(total, -32 * q)
    sums = classed[:, 0:OUTS]
    f, h1, h2 = f_ref[...], h1_ref[...], h2_ref[...]
    two_grad = dot(sums, w3_ref[...].astype(F32), ((1,), (0,)), HIGHEST) * (1.0 - h2 * h2)
    one_grad = dot(two_grad, w2_ref[...].astype(F32), ((1,), (1,)), HIGHEST) * (1.0 - h1 * h1)
    feature_grad = dot(one_grad, w1_ref[...].astype(F32), ((1,), (1,)), HIGHEST)
    three_ref[...] = dot(sums, h2, ((0,), (0,)), HIGHEST)
    two_ref[...] = dot(h1, two_grad, ((0,), (0,)), HIGHEST)
    one_ref[...] = dot(f, one_grad, ((0,), (0,)), HIGHEST)
    embed_ref[...] = feature_grad
    scale = scale_ref[...].astype(F32) * (1.0 / 64.0)
    time_ref[...] = scale[0] * jnp.sum(feature_grad, axis=0)


def shift(x, axis, step):
    size = lax.axis_size(axis)
    pairs = [(i, i + step) for i in range(size) if 0 <= i + step < size]
    return lax.ppermute(x, axis, pairs)


def spread(x, axis):
    size = lax.axis_size(axis)
    return lax.all_to_all(jnp.broadcast_to(x[None], (size,) + x.shape), axis, 0, 0, tiled=True)


def body(classes, check_index, snapshot, payoff, sensitivity, embed, time_vec, w_one, w_two, w_three):
    sd = jax.ShapeDtypeStruct
    tile = sd((GOALS, ROWS, COLS), BF16)
    to_down, to_up = vmem_call(
        edge_kernel,
        (tile, tile),
        [pltpu.VMEM((ROWS, COLS), F32)] * 2
        + [pltpu.VMEM((GOALS, ROWS, COLS), BF16)] * 3
        + [pltpu.VMEM((ROWS, COLS), jnp.int32), pltpu.SemaphoreType.DMA((4,))],
        source=pl.ANY,
    )(
        snapshot, payoff, sensitivity, classes
    )
    up = shift(to_down, "row", 1)
    down = shift(to_up, "row", -1)

    scale = jnp.broadcast_to(check_index.reshape(1, 1), (1, 64))
    layer = sd((CLASSES, 64), F32)
    table, feature, one, two = vmem_call(
        table_kernel, (sd((72, COLS), F32), layer, layer, layer), [pltpu.VMEM((32, COLS), F32)]
    )(scale, embed, time_vec.reshape(1, -1), w_one, w_two, w_three.T)

    ext = pltpu.VMEM((GOALS, EXT, COLS), F32)
    plane = pltpu.VMEM((EXT, COLS), F32)
    edge = sd((OCT + 1, 32, COLS), BF16)
    to_right, to_left = vmem_call(strip_kernel, (edge, edge), [ext, ext, ext, plane])(
        snapshot, payoff, sensitivity, classes, up, down
    )
    left = shift(to_right, "col", 1)
    right = shift(to_left, "col", -1)

    strip = pltpu.VMEM((OCT, EXT, COLS), F32)

    def many(*shape):
        return pltpu.VMEM(shape + (COLS,), F32)

    n = ACTIONS * POINTS
    snap, pay, sums = vmem_call(
        main_kernel,
        (tile, tile, sd((4, COLS), F32)),
        [
            many(ITERS, GOALS, EXT), ext, ext, plane,
            many(ITERS, OCT, EXT), strip, strip, plane,
            many(n, EXT), many(n, EXT), many(ACTIONS, EXT), many(ACTIONS, EXT), plane, plane, many(n, ROWS),
            many(ITERS, ACTIONS, GOALS, EXT), many(ITERS, ACTIONS, OCT, EXT),
            many(ITERS, GOALS, EXT), many(ITERS, GOALS, EXT),
            many(2, POINTS, GOALS, EXT), many(2, POINTS, OCT, EXT),
            many(OUTS, ROWS), many(GOALS, ROWS), many(GOALS, ROWS),
        ],
    )(snapshot, payoff, sensitivity, classes, up, down, left, right, table)

    sums = jnp.sum(spread(sums, "row"), axis=0)
    parts = spread(sums, "col")
    factor = 1.0 / math.sqrt(ROWS * lax.axis_size("row") * COLS * lax.axis_size("col"))

    def last(*refs):
        last_kernel(*refs, factor=factor)

    grads = vmem_call(
        last, (layer, sd((64,), F32), sd((64, 64), F32), sd((64, 64), F32), sd((OUTS, 64), F32)),
        [pltpu.VMEM((CLASSES, COLS), F32)],
    )(parts, scale, feature, one, two, w_one, w_two, w_three.T)
    return (snap, pay, grads[0], grads[1], grads[2], grads[3], grads[4].T)


def solution(mesh):
    tiled = P(None, "row", "col")
    return jax.shard_map(
        body,
        mesh=mesh,
        in_specs=(P("row", "col"), P(), tiled, tiled, tiled, P(), P(), P(), P(), P()),
        out_specs=(tiled, tiled, P(), P(), P(), P(), P()),
        check_vma=False,
    )
```

```python
import math

import jax
import jax.numpy as jnp
from jax import lax
from jax.experimental import pallas as pl
from jax.experimental.pallas import tpu as pltpu
from jax.sharding import PartitionSpec as P

ITERS = 3
ACTIONS = 4
POINTS = 5
OUTS = 24
GOALS = 24
CLASSES = 16
ROWS = 16
COLS = 128
DECAY = 0.9
SLACK = 0.05
VH, RH, FH = 6, 5, 3
TOP = 16
EXT = 48
GROUP = 16
OCT = GOALS // 8
HIGHEST = lax.Precision.HIGHEST
F32 = jnp.float32
BF16 = jnp.bfloat16


def vmem_call(kernel, out_shape, scratch=(), limit=40 * 1024 * 1024, source=pltpu.VMEM):
    whole = pl.BlockSpec(memory_space=pltpu.VMEM)
    given = pl.BlockSpec(memory_space=source)
    return lambda *args: pl.pallas_call(
        kernel,
        out_shape=out_shape,
        in_specs=[given] * len(args),
        out_specs=jax.tree.map(lambda _: whole, out_shape),
        scratch_shapes=list(scratch),
        compiler_params=pltpu.CompilerParams(vmem_limit_bytes=limit),
    )(*args)


def fetch(pairs, sems):
    copies = [pltpu.make_async_copy(a, b, sems.at[i]) for i, (a, b) in enumerate(pairs)]
    for copy in copies:
        copy.start()
    for copy in copies:
        copy.wait()


def lane_iota(shape):
    return lax.broadcasted_iota(jnp.int32, shape, len(shape) - 1)


def turn(x, shift):
    shift = shift % COLS
    return x if shift == 0 else pltpu.roll(x, shift, 1)


def dot(a, b, dims, precision=None):
    return lax.dot_general(a, b, (dims, ((), ())), precision=precision, preferred_element_type=F32)


def table_kernel(scale_hbm, embed_hbm, time_hbm, w1_hbm, w2_hbm, w3_hbm, tab_ref, f_ref, h1_ref, h2_ref,
                 scale_ref, w1_ref, w2_ref, w3_ref, raw, embed_ref, time_ref, sems):
    fetch(((scale_hbm, scale_ref), (embed_hbm, embed_ref), (time_hbm, time_ref),
           (w1_hbm, w1_ref), (w2_hbm, w2_ref), (w3_hbm, w3_ref)), sems)
    scale = scale_ref[...].astype(F32) * (1.0 / 64.0)
    feature = (embed_ref[...].astype(F32) + scale * time_ref[...].astype(F32)).astype(BF16)
    one = jnp.tanh(dot(feature, w1_ref[...], ((1,), (0,)))).astype(BF16)
    two = jnp.tanh(dot(one, w2_ref[...], ((1,), (0,)))).astype(BF16)
    f_ref[...] = feature.astype(F32)
    h1_ref[...] = one.astype(F32)
    h2_ref[...] = two.astype(F32)
    logits = dot(w3_ref[...], two, ((1,), (1,)))
    raw[...] = jnp.zeros_like(raw)
    tab_ref[...] = jnp.zeros_like(tab_ref)
    for a in range(ACTIONS):
        raw[8 * a : 8 * a + POINTS, 0:CLASSES] = logits[a * POINTS : (a + 1) * POINTS]
    valid = lax.broadcasted_iota(jnp.int32, (8, COLS), 0) < POINTS
    for a in range(ACTIONS):
        x = raw[8 * a : 8 * a + 8, :]
        weight = jnp.maximum(x, 0.0) + jnp.log(1.0 + jnp.exp(-jnp.abs(x))) + SLACK
        total = jnp.sum(jnp.where(valid, weight, 0.0), axis=0, keepdims=True)
        tab_ref[16 * a : 16 * a + 8, :] = DECAY * weight / total
        tab_ref[16 * a + 8 : 16 * a + 16, :] = 1.0 / ((1.0 + jnp.exp(-x)) * total)
    tab_ref[64:68, 0:CLASSES] = logits[ACTIONS * POINTS :]


def chance_row(a, k):
    return 16 * a + k


def slope_row(a, k):
    return 16 * a + 8 + k


def bonus_row(a):
    return 64 + a


def edge_kernel(all_ref, to_down, to_up, low, high):
    low[...] = jnp.zeros_like(low)
    high[...] = jnp.zeros_like(high)
    marked = all_ref[3 * GOALS].astype(F32)
    for g in range(GOALS):
        v, r, s = [all_ref[i * GOALS + g].astype(F32) for i in range(3)]
        low[0:6, :], low[6:11, :], low[11:14, :] = v[ROWS - VH :], r[ROWS - RH :], s[ROWS - FH :]
        high[0:6, :], high[6:11, :], high[11:14, :] = v[0:VH], r[0:RH], s[0:FH]
        if g < RH:
            low[14:15, :], high[14:15, :] = marked[ROWS - RH + g : ROWS - RH + g + 1], marked[g : g + 1]
        to_down[g] = low[...].astype(BF16)
        to_up[g] = high[...].astype(BF16)


def fill_rows(dst, g, up, mid, down, n):
    dst[g, TOP - n : TOP, :] = up
    dst[g, TOP : TOP + ROWS, :] = mid
    dst[g, TOP + ROWS : TOP + ROWS + n, :] = down


def extend_rows(all_ref, up_ref, down_ref, val, rew, sen, cls):
    def one(g, carry):
        up = up_ref[g].astype(F32)
        down = down_ref[g].astype(F32)
        fill_rows(val, g, up[0:6], all_ref[g].astype(F32), down[0:6], VH)
        fill_rows(rew, g, up[6:11], all_ref[GOALS + g].astype(F32), down[6:11], RH)
        fill_rows(sen, g, up[11:14], all_ref[2 * GOALS + g].astype(F32), down[11:14], FH)
        return carry

    lax.fori_loop(0, GOALS, one, 0, unroll=4)
    cls[...] = jnp.zeros_like(cls)
    cls[TOP : TOP + ROWS, :] = all_ref[3 * GOALS].astype(F32)
    for i in range(RH):
        cls[TOP - RH + i : TOP - RH + i + 1, :] = up_ref[i, 14:15, :].astype(F32)
        cls[TOP + ROWS + i : TOP + ROWS + i + 1, :] = down_ref[i, 14:15, :].astype(F32)


def strip_kernel(all_ref, up_ref, down_ref, tab_ref, to_right, to_left, val, rew, sen, cls):
    extend_rows(all_ref, up_ref, down_ref, val, rew, sen, cls)
    group_lane = lane_iota((8, COLS)) % GROUP
    group_at = lane_iota((8, COLS)) // GROUP

    def octet(o, carry):
        for j in range(4):
            rows = slice(8 + 8 * j, 16 + 8 * j)
            right = jnp.zeros((8, COLS), F32)
            left = jnp.zeros((8, COLS), F32)
            for q in range(8):
                p = GROUP * q
                v, r, s = val[o * 8 + q, rows, :], rew[o * 8 + q, rows, :], sen[o * 8 + q, rows, :]
                here = group_at == q
                part = jnp.where(group_lane < 11, turn(r, p + 11), turn(s, p + 14))
                right = jnp.where(here, jnp.where(group_lane < 6, turn(v, p + 6), part), right)
                part = jnp.where(group_lane < 11, turn(r, p + 6), turn(s, p + 11))
                left = jnp.where(here, jnp.where(group_lane < 6, turn(v, p), part), left)
            to_right[o, 8 * j : 8 * j + 8, :] = right.astype(to_right.dtype)
            to_left[o, 8 * j : 8 * j + 8, :] = left.astype(to_left.dtype)
        return carry

    lax.fori_loop(0, OCT, octet, 0)
    for j in range(4):
        c = cls[8 + 8 * j : 16 + 8 * j, :]
        right = jnp.zeros((8, COLS), F32)
        left = jnp.zeros((8, COLS), F32)
        for q in range(8):
            here = group_at == q
            right = jnp.where(here, turn(c, GROUP * q + 6), right)
            left = jnp.where(here, turn(c, GROUP * q), left)
        to_right[OCT, 8 * j : 8 * j + 8, :] = right.astype(to_right.dtype)
        to_left[OCT, 8 * j : 8 * j + 8, :] = left.astype(to_left.dtype)


def look_up(base, cls, tab_ref, chance, bonus, mask, slope=None):
    at = slice(base, base + 8)
    number = cls[at, :].astype(jnp.int32)
    inside = number > 0
    which = jnp.maximum(number - 1, 0)
    mask[at, :] = inside.astype(F32)

    def look(row):
        table = jnp.broadcast_to(tab_ref[row : row + 1, :], (8, COLS))
        return jnp.where(inside, jnp.take_along_axis(table, which, axis=1), 0.0)

    for a in range(ACTIONS):
        for k in range(POINTS):
            chance[a * POINTS + k, at, :] = look(chance_row(a, k))
            if slope is not None:
                slope[a * POINTS + k, base - TOP : base - TOP + 8, :] = look(slope_row(a, k))
        bonus[a, at, :] = look(bonus_row(a))


def map_kernel(cls, tab_ref, chance, bonus, mask, slope):
    for j in range(4):
        look_up(8 + 8 * j, cls, tab_ref, chance, bonus, mask, slope if j in (1, 2) else None)


def main_kernel(val0, rew, sen, cls, chance, bonus, mask, slope, lb_ref, rb_ref, tab_ref,
                snap_ref, pay_ref, sums_ref,
                later, sval, srew, ssen, scls, schance, sbonus, smask,
                soft, ssoft, lshift, rshift, push, spush, adjoint, cgrad, paysum, packed):
    val = [val0, later.at[0], later.at[1]]
    lane = lane_iota((8, COLS))
    glane = lane % GROUP
    inner = glane < 6
    first, last = lane == 0, lane == COLS - 1
    strip_first, strip_last = glane == 5, glane == 6
    for o in range(OCT + 1):
        for j in range(4):
            left = lb_ref[o, 8 * j : 8 * j + 8, :].astype(F32)
            right = rb_ref[o, 8 * j : 8 * j + 8, :].astype(F32)
            at = slice(8 + 8 * j, 16 + 8 * j)
            outer = jnp.where(inner, left, turn(right, 6))
            if o == OCT:
                scls[at, :] = jnp.where(glane < 12, outer, 0.0)
            else:
                sval[0, o, at, :] = outer
                srew[o, at, :] = jnp.where(inner, turn(left, -5), right)
                ssen[o, at, :] = jnp.where(inner, turn(left, -8), turn(right, -5))
    for j in range(4):
        look_up(8 + 8 * j, scls, tab_ref, schance, sbonus, smask)

    def where_tile(start):
        base = TOP + start
        return slice(base, base + 8), slice(base - 1, base + 7), slice(base + 1, base + 9)

    def soft_step(near, reward, ch, bo, keep_value):
        q = []
        for a in range(ACTIONS):
            total = reward + bo[a]
            for k in range(POINTS):
                total = total + ch[a * POINTS + k] * near[k]
            q.append(total)
        highest = jnp.maximum(jnp.maximum(q[0], q[1]), jnp.maximum(q[2], q[3]))
        e = [jnp.exp(x - highest) for x in q]
        total = (e[0] + e[1]) + (e[2] + e[3])
        inverse = 1.0 / total
        value = highest + jnp.log(total) if keep_value else None
        return [x * inverse for x in e], value

    for t in range(ITERS):
        keep = t < ITERS - 1

        def forward(o, start, t=t, keep=keep):
            rows, above, below = where_tile(start)
            ch = [chance[n, rows, :] for n in range(ACTIONS * POINTS)]
            bo = [bonus[a, rows, :] for a in range(ACTIONS)]
            sv = sval[t, o, rows, :]
            edge = jnp.zeros((8, COLS), F32)
            for q in range(8):
                p, g = GROUP * q, o * 8 + q
                x = val[t][g, rows, :]
                fill = turn(sv, -(p + 6))
                toleft = turn(jnp.where(last, fill, x), 1)
                toright = turn(jnp.where(first, fill, x), -1)
                edge = jnp.where((lane == p + 5) | (lane == p + 6), turn(x, p + 6), edge)
                lshift[t, g, rows, :] = toleft
                rshift[t, g, rows, :] = toright
                near = [x, val[t][g, above, :], val[t][g, below, :], toleft, toright]
                probs, value = soft_step(near, rew[g, rows, :], ch, bo, keep)
                for a in range(ACTIONS):
                    soft[t, a, g, rows, :] = probs[a]
                if keep:
                    val[t + 1][g, rows, :] = value * mask[rows, :]
            near = [sv, sval[t, o, above, :], sval[t, o, below, :],
                    turn(jnp.where(strip_first, edge, sv), 1), turn(jnp.where(strip_last, edge, sv), -1)]
            ch = [schance[n, rows, :] for n in range(ACTIONS * POINTS)]
            bo = [sbonus[a, rows, :] for a in range(ACTIONS)]
            probs, value = soft_step(near, srew[o, rows, :], ch, bo, keep)
            for a in range(ACTIONS):
                ssoft[t, a, o, rows, :] = probs[a]
            if keep:
                sval[t + 1, o, rows, :] = value * smask[rows, :]

        starts = (-6, 2, 10, 18) if t == 0 else (-4, 4, 12)

        def forward_all(o, carry, forward=forward, starts=starts):
            for start in starts:
                forward(o, start)
            return carry

        lax.fori_loop(0, OCT, forward_all, 0)

    cgrad[...] = jnp.zeros_like(cgrad)
    paysum[...] = jnp.zeros_like(paysum)

    def gather(o, rows, above, below, old):
        s3, s4 = spush[old, 3, o, rows, :], spush[old, 4, o, rows, :]
        both = jnp.where(strip_last, s3, s4)
        edge = jnp.zeros((8, COLS), F32)
        out = []
        for q in range(8):
            p, g = GROUP * q, o * 8 + q
            p3, p4 = push[old, 3, g, rows, :], push[old, 4, g, rows, :]
            fill = turn(both, -(p + 6))
            from_right = turn(jnp.where(first, fill, p3), -1)
            from_left = turn(jnp.where(last, fill, p4), 1)
            edge = jnp.where((lane == p + 5) | (lane == p + 6), turn(jnp.where(first, p3, p4), p + 6), edge)
            out.append(push[old, 0, g, rows, :] + push[old, 1, g, below, :] + push[old, 2, g, above, :]
                       + from_right + from_left)
        strip = (spush[old, 0, o, rows, :] + spush[old, 1, o, below, :] + spush[old, 2, o, above, :]
                 + turn(jnp.where(strip_last, edge, s3), -1) + turn(jnp.where(strip_first, edge, s4), 1))
        return out, strip

    for t in reversed(range(ITERS)):
        new, old = t % 2, (t + 1) % 2

        def spread_out(o, start, t=t, new=new, old=old):
            rows, above, below = where_tile(start)
            if t == ITERS - 1:
                adj = [sen[o * 8 + q, rows, :] for q in range(8)]
                strip = ssen[o, rows, :]
            else:
                adj, strip = gather(o, rows, above, below, old)
                for q in range(8):
                    adjoint[o * 8 + q, rows, :] = adj[q]
            for q in range(8):
                g = o * 8 + q
                grads = [adj[q] * soft[t, a, g, rows, :] for a in range(ACTIONS)]
                for k in range(POINTS):
                    total = grads[0] * chance[k, rows, :]
                    for a in range(1, ACTIONS):
                        total = total + grads[a] * chance[a * POINTS + k, rows, :]
                    push[new, k, g, rows, :] = total
            grads = [strip * ssoft[t, a, o, rows, :] for a in range(ACTIONS)]
            for k in range(POINTS):
                total = grads[0] * schance[k, rows, :]
                for a in range(1, ACTIONS):
                    total = total + grads[a] * schance[a * POINTS + k, rows, :]
                spush[new, k, o, rows, :] = total

        def collect(o, start, t=t):
            rows, above, below = where_tile(start)
            source = sen if t == ITERS - 1 else adjoint
            adj = [source[o * 8 + q, rows, :] for q in range(8)]
            at = slice(start, start + 8)
            for q in range(8):
                g = o * 8 + q
                grads = [adj[q] * soft[t, a, g, rows, :] for a in range(ACTIONS)]
                paysum[g, at, :] += (grads[0] + grads[1]) + (grads[2] + grads[3])
            for a in range(ACTIONS):
                sums = [cgrad[a * POINTS + k, at, :] for k in range(POINTS)]
                total = cgrad[ACTIONS * POINTS + a, at, :]
                for q in range(8):
                    g = o * 8 + q
                    grad = adj[q] * soft[t, a, g, rows, :]
                    total = total + grad
                    near = [val[t][g, rows, :], val[t][g, above, :], val[t][g, below, :],
                            lshift[t, g, rows, :], rshift[t, g, rows, :]]
                    sums = [x + grad * y for x, y in zip(sums, near)]
                for k in range(POINTS):
                    cgrad[a * POINTS + k, at, :] = sums[k]
                cgrad[ACTIONS * POINTS + a, at, :] = total

        def backward_all(o, carry, spread_out=spread_out, collect=collect):
            for start in (-4, 4, 12):
                spread_out(o, start)
            for start in (0, 8):
                collect(o, start)
            return carry

        lax.fori_loop(0, OCT, backward_all, 0)

    def finish(o, carry):
        for start in (0, 8):
            rows, above, below = where_tile(start)
            adj = gather(o, rows, above, below, 0)[0]
            for q in range(8):
                packed[o * 8 + q, start : start + 8, :] = adj[q]
        return carry

    lax.fori_loop(0, OCT, finish, 0)
    snap_ref[...] = packed[...].astype(BF16)
    pay_ref[...] = paysum[...].astype(BF16)
    for j in range(2):
        at = slice(8 * j, 8 * j + 8)
        rows = slice(TOP + 8 * j, TOP + 8 * j + 8)
        for a in range(ACTIONS):
            grads = [cgrad[a * POINTS + k, at, :] for k in range(POINTS)]
            weighted = grads[0] * chance[a * POINTS, rows, :]
            for k in range(1, POINTS):
                weighted = weighted + grads[k] * chance[a * POINTS + k, rows, :]
            for k in range(POINTS):
                cgrad[a * POINTS + k, at, :] = (DECAY * grads[k] - weighted) * slope[a * POINTS + k, at, :]
    number = lax.broadcasted_iota(jnp.int32, (CLASSES, COLS), 0)
    total = jnp.zeros((CLASSES, OUTS), F32)
    which = cls[TOP : TOP + ROWS, :].astype(jnp.int32) - 1
    for i in range(ROWS):
        one_hot = (number == which[i : i + 1]).astype(BF16)
        total = total + dot(one_hot, cgrad[:, i, :].astype(BF16), ((1,), (1,)))
    packed[0, :, :] = jnp.zeros((ROWS, COLS), F32)
    packed[0, 0:CLASSES, 0:OUTS] = total
    parts = [packed[0, 4 * q : 4 * q + 4, :] for q in range(4)]
    sums_ref[...] = (parts[0] + turn(parts[1], 32)) + (turn(parts[2], 64) + turn(parts[3], 96))


def last_kernel(parts_ref, scale_ref, f_ref, h1_ref, h2_ref, w1_ref, w2_ref, w3_ref,
                embed_ref, time_ref, one_ref, two_ref, three_ref, classed, *, factor):
    total = parts_ref[0]
    for i in range(1, parts_ref.shape[0]):
        total = total + parts_ref[i]
    total = total * factor
    for q in range(4):
        classed[4 * q : 4 * q + 4, :] = turn(total, -32 * q)
    sums = classed[:, 0:OUTS]
    f, h1, h2 = f_ref[...], h1_ref[...], h2_ref[...]
    two_grad = dot(sums, w3_ref[...].astype(F32), ((1,), (0,)), HIGHEST) * (1.0 - h2 * h2)
    one_grad = dot(two_grad, w2_ref[...].astype(F32), ((1,), (1,)), HIGHEST) * (1.0 - h1 * h1)
    feature_grad = dot(one_grad, w1_ref[...].astype(F32), ((1,), (1,)), HIGHEST)
    three_ref[...] = dot(sums, h2, ((0,), (0,)), HIGHEST)
    two_ref[...] = dot(h1, two_grad, ((0,), (0,)), HIGHEST)
    one_ref[...] = dot(f, one_grad, ((0,), (0,)), HIGHEST)
    embed_ref[...] = feature_grad
    scale = scale_ref[...].astype(F32) * (1.0 / 64.0)
    time_ref[...] = scale[0] * jnp.sum(feature_grad, axis=0)


def shift(x, axis, step):
    size = lax.axis_size(axis)
    pairs = [(i, i + step) for i in range(size) if 0 <= i + step < size]
    return lax.ppermute(x, axis, pairs)


def spread(x, axis):
    size = lax.axis_size(axis)
    return lax.all_to_all(jnp.broadcast_to(x[None], (size,) + x.shape), axis, 0, 0, tiled=True)


def body(classes, check_index, snapshot, payoff, sensitivity, embed, time_vec, w_one, w_two, w_three):
    sd = jax.ShapeDtypeStruct
    tile = sd((GOALS, ROWS, COLS), BF16)
    marked = (classes + 1).astype(BF16)[None]
    everything = jnp.concatenate([snapshot, payoff, sensitivity, marked], axis=0)
    to_down, to_up = vmem_call(edge_kernel, (tile, tile), [pltpu.VMEM((ROWS, COLS), F32)] * 2)(everything)
    up = shift(to_down, "row", 1)
    down = shift(to_up, "row", -1)

    scale = jnp.broadcast_to(check_index.reshape(1, 1), (1, 64))
    layer = sd((CLASSES, 64), F32)
    square = sd((64, 64), BF16)
    table, feature, one, two, scale, w_one, w_two, w_three = vmem_call(
        table_kernel,
        (sd((72, COLS), F32), layer, layer, layer, sd((1, 64), jnp.int32), square, square, sd((OUTS, 64), BF16)),
        [pltpu.VMEM((32, COLS), F32), pltpu.VMEM((CLASSES, 64), BF16), pltpu.VMEM((1, 64), BF16),
         pltpu.SemaphoreType.DMA((6,))],
        source=pltpu.HBM,
    )(scale, embed, time_vec.reshape(1, -1), w_one, w_two, w_three.T)

    plane = pltpu.VMEM((EXT, COLS), F32)
    edge = sd((OCT + 1, 32, COLS), BF16)
    ext = sd((GOALS, EXT, COLS), F32)
    to_right, to_left, val, rew, sen, cls = vmem_call(
        strip_kernel, (edge, edge, ext, ext, ext, sd((EXT, COLS), F32))
    )(everything, up, down, table)
    left = shift(to_right, "col", 1)
    right = shift(to_left, "col", -1)

    strip = pltpu.VMEM((OCT, EXT, COLS), F32)

    def many(*shape):
        return pltpu.VMEM(shape + (COLS,), F32)

    n = ACTIONS * POINTS
    chance, bonus, mask, slope = vmem_call(
        map_kernel,
        (sd((n, EXT, COLS), F32), sd((ACTIONS, EXT, COLS), F32), sd((EXT, COLS), F32), sd((n, ROWS, COLS), F32)),
    )(cls, table)
    snap, pay, sums = vmem_call(
        main_kernel,
        (tile, tile, sd((4, COLS), F32)),
        [
            many(ITERS - 1, GOALS, EXT), many(ITERS, OCT, EXT), strip, strip, plane,
            many(n, EXT), many(ACTIONS, EXT), plane,
            many(ITERS, ACTIONS, GOALS, EXT), many(ITERS, ACTIONS, OCT, EXT),
            many(ITERS, GOALS, EXT), many(ITERS, GOALS, EXT),
            many(2, POINTS, GOALS, EXT), many(2, POINTS, OCT, EXT), many(GOALS, EXT),
            many(OUTS, ROWS), many(GOALS, ROWS), many(GOALS, ROWS),
        ],
    )(val, rew, sen, cls, chance, bonus, mask, slope, left, right, table)

    sums = jnp.sum(spread(sums, "row"), axis=0)
    parts = spread(sums, "col")
    factor = 1.0 / math.sqrt(ROWS * lax.axis_size("row") * COLS * lax.axis_size("col"))

    def last(*refs):
        last_kernel(*refs, factor=factor)

    grads = vmem_call(
        last, (layer, sd((64,), F32), sd((64, 64), F32), sd((64, 64), F32), sd((OUTS, 64), F32)),
        [pltpu.VMEM((CLASSES, COLS), F32)],
    )(parts, scale, feature, one, two, w_one, w_two, w_three)
    return (snap, pay, grads[0], grads[1], grads[2], grads[3], grads[4].T)


def solution(mesh):
    tiled = P(None, "row", "col")
    return jax.shard_map(
        body,
        mesh=mesh,
        in_specs=(P("row", "col"), P(), tiled, tiled, tiled, P(), P(), P(), P(), P()),
        out_specs=(tiled, tiled, P(), P(), P(), P(), P()),
        check_vma=False,
    )
```

```python
import math

import jax
import jax.numpy as jnp
from jax import lax
from jax.experimental import pallas as pl
from jax.experimental.pallas import tpu as pltpu
from jax.sharding import PartitionSpec as P

ITERS = 3
ACTIONS = 4
POINTS = 5
OUTS = 24
GOALS = 24
CLASSES = 16
ROWS = 16
COLS = 128
DECAY = 0.9
SLACK = 0.05
VH, RH, FH = 6, 5, 3
TOP = 16
EXT = 48
GROUP = 16
OCT = GOALS // 8
HIGHEST = lax.Precision.HIGHEST
F32 = jnp.float32
BF16 = jnp.bfloat16


def vmem_call(kernel, out_shape, scratch=(), limit=40 * 1024 * 1024, source=pltpu.VMEM):
    whole = pl.BlockSpec(memory_space=pltpu.VMEM)
    given = pl.BlockSpec(memory_space=source)
    return lambda *args: pl.pallas_call(
        kernel,
        out_shape=out_shape,
        in_specs=[given] * len(args),
        out_specs=jax.tree.map(lambda _: whole, out_shape),
        scratch_shapes=list(scratch),
        compiler_params=pltpu.CompilerParams(vmem_limit_bytes=limit),
    )(*args)


def fetch(pairs, sems):
    copies = [pltpu.make_async_copy(a, b, sems.at[i]) for i, (a, b) in enumerate(pairs)]
    for copy in copies:
        copy.start()
    for copy in copies:
        copy.wait()


def lane_iota(shape):
    return lax.broadcasted_iota(jnp.int32, shape, len(shape) - 1)


def turn(x, shift):
    shift = shift % COLS
    return x if shift == 0 else pltpu.roll(x, shift, 1)


def dot(a, b, dims, precision=None):
    return lax.dot_general(a, b, (dims, ((), ())), precision=precision, preferred_element_type=F32)


def table_kernel(scale_hbm, embed_hbm, time_hbm, w1_hbm, w2_hbm, w3_hbm, tab_ref, f_ref, h1_ref, h2_ref,
                 scale_ref, w1_ref, w2_ref, w3_ref, raw, embed_ref, time_ref, sems):
    fetch(((scale_hbm, scale_ref), (embed_hbm, embed_ref), (time_hbm, time_ref),
           (w1_hbm, w1_ref), (w2_hbm, w2_ref), (w3_hbm, w3_ref)), sems)
    scale = scale_ref[...].astype(F32) * (1.0 / 64.0)
    feature = (embed_ref[...].astype(F32) + scale * time_ref[...].astype(F32)).astype(BF16)
    one = jnp.tanh(dot(feature, w1_ref[...], ((1,), (0,)))).astype(BF16)
    two = jnp.tanh(dot(one, w2_ref[...], ((1,), (0,)))).astype(BF16)
    f_ref[...] = feature.astype(F32)
    h1_ref[...] = one.astype(F32)
    h2_ref[...] = two.astype(F32)
    logits = dot(w3_ref[...], two, ((1,), (1,)))
    raw[...] = jnp.zeros_like(raw)
    tab_ref[...] = jnp.zeros_like(tab_ref)
    for a in range(ACTIONS):
        raw[8 * a : 8 * a + POINTS, 0:CLASSES] = logits[a * POINTS : (a + 1) * POINTS]
    valid = lax.broadcasted_iota(jnp.int32, (8, COLS), 0) < POINTS
    for a in range(ACTIONS):
        x = raw[8 * a : 8 * a + 8, :]
        weight = jnp.maximum(x, 0.0) + jnp.log(1.0 + jnp.exp(-jnp.abs(x))) + SLACK
        total = jnp.sum(jnp.where(valid, weight, 0.0), axis=0, keepdims=True)
        tab_ref[16 * a : 16 * a + 8, :] = DECAY * weight / total
        tab_ref[16 * a + 8 : 16 * a + 16, :] = 1.0 / ((1.0 + jnp.exp(-x)) * total)
    tab_ref[64:68, 0:CLASSES] = logits[ACTIONS * POINTS :]


def chance_row(a, k):
    return 16 * a + k


def slope_row(a, k):
    return 16 * a + 8 + k


def bonus_row(a):
    return 64 + a


def edge_kernel(all_ref, to_down, to_up, low, high):
    low[...] = jnp.zeros_like(low)
    high[...] = jnp.zeros_like(high)
    marked = all_ref[3 * GOALS].astype(F32)
    for g in range(GOALS):
        v, r, s = [all_ref[i * GOALS + g].astype(F32) for i in range(3)]
        low[0:6, :], low[6:11, :], low[11:14, :] = v[ROWS - VH :], r[ROWS - RH :], s[ROWS - FH :]
        high[0:6, :], high[6:11, :], high[11:14, :] = v[0:VH], r[0:RH], s[0:FH]
        if g < RH:
            low[14:15, :], high[14:15, :] = marked[ROWS - RH + g : ROWS - RH + g + 1], marked[g : g + 1]
        to_down[g] = low[...].astype(BF16)
        to_up[g] = high[...].astype(BF16)


def fill_rows(dst, g, up, mid, down, n):
    dst[g, TOP - n : TOP, :] = up
    dst[g, TOP : TOP + ROWS, :] = mid
    dst[g, TOP + ROWS : TOP + ROWS + n, :] = down


def extend_rows(all_ref, up_ref, down_ref, val, rew, sen, cls):
    def one(g, carry):
        up = up_ref[g].astype(F32)
        down = down_ref[g].astype(F32)
        fill_rows(val, g, up[0:6], all_ref[g].astype(F32), down[0:6], VH)
        fill_rows(rew, g, up[6:11], all_ref[GOALS + g].astype(F32), down[6:11], RH)
        fill_rows(sen, g, up[11:14], all_ref[2 * GOALS + g].astype(F32), down[11:14], FH)
        return carry

    lax.fori_loop(0, GOALS, one, 0, unroll=4)
    cls[...] = jnp.zeros_like(cls)
    cls[TOP : TOP + ROWS, :] = all_ref[3 * GOALS].astype(F32)
    for i in range(RH):
        cls[TOP - RH + i : TOP - RH + i + 1, :] = up_ref[i, 14:15, :].astype(F32)
        cls[TOP + ROWS + i : TOP + ROWS + i + 1, :] = down_ref[i, 14:15, :].astype(F32)


def strip_kernel(all_ref, up_ref, down_ref, tab_ref, to_right, to_left, val, rew, sen, cls):
    extend_rows(all_ref, up_ref, down_ref, val, rew, sen, cls)
    group_lane = lane_iota((8, COLS)) % GROUP
    group_at = lane_iota((8, COLS)) // GROUP

    def octet(o, carry):
        for j in range(4):
            rows = slice(8 + 8 * j, 16 + 8 * j)
            right = jnp.zeros((8, COLS), F32)
            left = jnp.zeros((8, COLS), F32)
            for q in range(8):
                p = GROUP * q
                v, r, s = val[o * 8 + q, rows, :], rew[o * 8 + q, rows, :], sen[o * 8 + q, rows, :]
                here = group_at == q
                part = jnp.where(group_lane < 11, turn(r, p + 11), turn(s, p + 14))
                right = jnp.where(here, jnp.where(group_lane < 6, turn(v, p + 6), part), right)
                part = jnp.where(group_lane < 11, turn(r, p + 6), turn(s, p + 11))
                left = jnp.where(here, jnp.where(group_lane < 6, turn(v, p), part), left)
            to_right[o, 8 * j : 8 * j + 8, :] = right.astype(to_right.dtype)
            to_left[o, 8 * j : 8 * j + 8, :] = left.astype(to_left.dtype)
        return carry

    lax.fori_loop(0, OCT, octet, 0)
    for j in range(4):
        c = cls[8 + 8 * j : 16 + 8 * j, :]
        right = jnp.zeros((8, COLS), F32)
        left = jnp.zeros((8, COLS), F32)
        for q in range(8):
            here = group_at == q
            right = jnp.where(here, turn(c, GROUP * q + 6), right)
            left = jnp.where(here, turn(c, GROUP * q), left)
        to_right[OCT, 8 * j : 8 * j + 8, :] = right.astype(to_right.dtype)
        to_left[OCT, 8 * j : 8 * j + 8, :] = left.astype(to_left.dtype)


def look_up(base, cls, tab_ref, chance, bonus, mask, slope=None):
    at = slice(base, base + 8)
    number = cls[at, :].astype(jnp.int32)
    inside = number > 0
    which = jnp.maximum(number - 1, 0)
    mask[at, :] = inside.astype(F32)

    def look(row):
        table = jnp.broadcast_to(tab_ref[row : row + 1, :], (8, COLS))
        return jnp.where(inside, jnp.take_along_axis(table, which, axis=1), 0.0)

    for a in range(ACTIONS):
        for k in range(POINTS):
            chance[a * POINTS + k, at, :] = look(chance_row(a, k))
            if slope is not None:
                slope[a * POINTS + k, base - TOP : base - TOP + 8, :] = look(slope_row(a, k))
        bonus[a, at, :] = look(bonus_row(a))


def map_kernel(cls, tab_ref, chance, bonus, mask, slope):
    for j in range(4):
        look_up(8 + 8 * j, cls, tab_ref, chance, bonus, mask, slope if j in (1, 2) else None)


def main_kernel(val0, rew, sen, cls, chance, bonus, mask, slope, lb_ref, rb_ref, tab_ref,
                snap_ref, pay_ref, sums_ref,
                later, sval, srew, ssen, scls, schance, sbonus, smask,
                soft, ssoft, lshift, rshift, push, spush, adjoint, cgrad, paysum, packed):
    val = [val0, later.at[0], later.at[1]]
    lane = lane_iota((8, COLS))
    glane = lane % GROUP
    inner = glane < 6
    first, last = lane == 0, lane == COLS - 1
    strip_first, strip_last = glane == 5, glane == 6
    for o in range(OCT + 1):
        for j in range(4):
            left = lb_ref[o, 8 * j : 8 * j + 8, :].astype(F32)
            right = rb_ref[o, 8 * j : 8 * j + 8, :].astype(F32)
            at = slice(8 + 8 * j, 16 + 8 * j)
            outer = jnp.where(inner, left, turn(right, 6))
            if o == OCT:
                scls[at, :] = jnp.where(glane < 12, outer, 0.0)
            else:
                sval[0, o, at, :] = outer
                srew[o, at, :] = jnp.where(inner, turn(left, -5), right)
                ssen[o, at, :] = jnp.where(inner, turn(left, -8), turn(right, -5))
    for j in range(4):
        look_up(8 + 8 * j, scls, tab_ref, schance, sbonus, smask)

    def where_tile(start):
        base = TOP + start
        return slice(base, base + 8), slice(base - 1, base + 7), slice(base + 1, base + 9)

    def soft_step(near, reward, ch, bo, keep_value):
        q = []
        for a in range(ACTIONS):
            total = reward + bo[a]
            for k in range(POINTS):
                total = total + ch[a * POINTS + k] * near[k]
            q.append(total)
        highest = jnp.maximum(jnp.maximum(q[0], q[1]), jnp.maximum(q[2], q[3]))
        e = [jnp.exp(x - highest) for x in q]
        total = (e[0] + e[1]) + (e[2] + e[3])
        inverse = 1.0 / total
        value = highest + jnp.log(total) if keep_value else None
        return [x * inverse for x in e], value

    for t in range(ITERS):
        keep = t < ITERS - 1

        def forward(o, start, t=t, keep=keep):
            rows, above, below = where_tile(start)
            ch = [chance[n, rows, :] for n in range(ACTIONS * POINTS)]
            bo = [bonus[a, rows, :] for a in range(ACTIONS)]
            sv = sval[t, o, rows, :]
            edge = jnp.zeros((8, COLS), F32)
            for q in range(8):
                p, g = GROUP * q, o * 8 + q
                x = val[t][g, rows, :]
                fill = turn(sv, -(p + 6))
                toleft = turn(jnp.where(last, fill, x), 1)
                toright = turn(jnp.where(first, fill, x), -1)
                edge = jnp.where((lane == p + 5) | (lane == p + 6), turn(x, p + 6), edge)
                lshift[t, g, rows, :] = toleft
                rshift[t, g, rows, :] = toright
                near = [x, val[t][g, above, :], val[t][g, below, :], toleft, toright]
                probs, value = soft_step(near, rew[g, rows, :], ch, bo, keep)
                for a in range(ACTIONS):
                    soft[t, a, g, rows, :] = probs[a]
                if keep:
                    val[t + 1][g, rows, :] = value * mask[rows, :]
            near = [sv, sval[t, o, above, :], sval[t, o, below, :],
                    turn(jnp.where(strip_first, edge, sv), 1), turn(jnp.where(strip_last, edge, sv), -1)]
            ch = [schance[n, rows, :] for n in range(ACTIONS * POINTS)]
            bo = [sbonus[a, rows, :] for a in range(ACTIONS)]
            probs, value = soft_step(near, srew[o, rows, :], ch, bo, keep)
            for a in range(ACTIONS):
                ssoft[t, a, o, rows, :] = probs[a]
            if keep:
                sval[t + 1, o, rows, :] = value * smask[rows, :]

        starts = (-6, 2, 10, 18) if t == 0 else (-4, 4, 12)

        def forward_all(o, carry, forward=forward, starts=starts):
            for start in starts:
                forward(o, start)
            return carry

        lax.fori_loop(0, OCT, forward_all, 0)

    cgrad[...] = jnp.zeros_like(cgrad)
    paysum[...] = jnp.zeros_like(paysum)

    def gather(o, rows, above, below, old):
        s3, s4 = spush[old, 3, o, rows, :], spush[old, 4, o, rows, :]
        both = jnp.where(strip_last, s3, s4)
        edge = jnp.zeros((8, COLS), F32)
        out = []
        for q in range(8):
            p, g = GROUP * q, o * 8 + q
            p3, p4 = push[old, 3, g, rows, :], push[old, 4, g, rows, :]
            fill = turn(both, -(p + 6))
            from_right = turn(jnp.where(first, fill, p3), -1)
            from_left = turn(jnp.where(last, fill, p4), 1)
            edge = jnp.where((lane == p + 5) | (lane == p + 6), turn(jnp.where(first, p3, p4), p + 6), edge)
            out.append(push[old, 0, g, rows, :] + push[old, 1, g, below, :] + push[old, 2, g, above, :]
                       + from_right + from_left)
        strip = (spush[old, 0, o, rows, :] + spush[old, 1, o, below, :] + spush[old, 2, o, above, :]
                 + turn(jnp.where(strip_last, edge, s3), -1) + turn(jnp.where(strip_first, edge, s4), 1))
        return out, strip

    for t in reversed(range(ITERS)):
        new, old = t % 2, (t + 1) % 2

        def spread_out(o, start, t=t, new=new, old=old):
            rows, above, below = where_tile(start)
            if t == ITERS - 1:
                adj = [sen[o * 8 + q, rows, :] for q in range(8)]
                strip = ssen[o, rows, :]
            else:
                adj, strip = gather(o, rows, above, below, old)
                for q in range(8):
                    adjoint[o * 8 + q, rows, :] = adj[q]
            for q in range(8):
                g = o * 8 + q
                grads = [adj[q] * soft[t, a, g, rows, :] for a in range(ACTIONS)]
                for k in range(POINTS):
                    total = grads[0] * chance[k, rows, :]
                    for a in range(1, ACTIONS):
                        total = total + grads[a] * chance[a * POINTS + k, rows, :]
                    push[new, k, g, rows, :] = total
            grads = [strip * ssoft[t, a, o, rows, :] for a in range(ACTIONS)]
            for k in range(POINTS):
                total = grads[0] * schance[k, rows, :]
                for a in range(1, ACTIONS):
                    total = total + grads[a] * schance[a * POINTS + k, rows, :]
                spush[new, k, o, rows, :] = total

        def collect(o, start, t=t):
            rows, above, below = where_tile(start)
            source = sen if t == ITERS - 1 else adjoint
            adj = [source[o * 8 + q, rows, :] for q in range(8)]
            at = slice(start, start + 8)
            for q in range(8):
                g = o * 8 + q
                grads = [adj[q] * soft[t, a, g, rows, :] for a in range(ACTIONS)]
                paysum[g, at, :] += (grads[0] + grads[1]) + (grads[2] + grads[3])
            for a in range(ACTIONS):
                sums = [cgrad[a * POINTS + k, at, :] for k in range(POINTS)]
                total = cgrad[ACTIONS * POINTS + a, at, :]
                for q in range(8):
                    g = o * 8 + q
                    grad = adj[q] * soft[t, a, g, rows, :]
                    total = total + grad
                    near = [val[t][g, rows, :], val[t][g, above, :], val[t][g, below, :],
                            lshift[t, g, rows, :], rshift[t, g, rows, :]]
                    sums = [x + grad * y for x, y in zip(sums, near)]
                for k in range(POINTS):
                    cgrad[a * POINTS + k, at, :] = sums[k]
                cgrad[ACTIONS * POINTS + a, at, :] = total

        def backward_all(o, carry, spread_out=spread_out, collect=collect):
            for start in (-4, 4, 12):
                spread_out(o, start)
            for start in (0, 8):
                collect(o, start)
            return carry

        lax.fori_loop(0, OCT, backward_all, 0)

    def finish(o, carry):
        for start in (0, 8):
            rows, above, below = where_tile(start)
            adj = gather(o, rows, above, below, 0)[0]
            for q in range(8):
                packed[o * 8 + q, start : start + 8, :] = adj[q]
        return carry

    lax.fori_loop(0, OCT, finish, 0)
    snap_ref[...] = packed[...].astype(BF16)
    pay_ref[...] = paysum[...].astype(BF16)
    for j in range(2):
        at = slice(8 * j, 8 * j + 8)
        rows = slice(TOP + 8 * j, TOP + 8 * j + 8)
        for a in range(ACTIONS):
            grads = [cgrad[a * POINTS + k, at, :] for k in range(POINTS)]
            weighted = grads[0] * chance[a * POINTS, rows, :]
            for k in range(1, POINTS):
                weighted = weighted + grads[k] * chance[a * POINTS + k, rows, :]
            for k in range(POINTS):
                cgrad[a * POINTS + k, at, :] = (DECAY * grads[k] - weighted) * slope[a * POINTS + k, at, :]
    number = lax.broadcasted_iota(jnp.int32, (CLASSES, COLS), 0)
    total = jnp.zeros((CLASSES, OUTS), F32)
    which = cls[TOP : TOP + ROWS, :].astype(jnp.int32) - 1
    for i in range(ROWS):
        one_hot = (number == which[i : i + 1]).astype(BF16)
        total = total + dot(one_hot, cgrad[:, i, :].astype(BF16), ((1,), (1,)))
    packed[0, :, :] = jnp.zeros((ROWS, COLS), F32)
    packed[0, 0:CLASSES, 0:OUTS] = total
    parts = [packed[0, 4 * q : 4 * q + 4, :] for q in range(4)]
    sums_ref[...] = (parts[0] + turn(parts[1], 32)) + (turn(parts[2], 64) + turn(parts[3], 96))


def last_kernel(parts_ref, scale_ref, f_ref, h1_ref, h2_ref, w1_ref, w2_ref, w3_ref,
                embed_ref, time_ref, one_ref, two_ref, three_ref, classed, *, factor):
    total = parts_ref[0]
    for i in range(1, parts_ref.shape[0]):
        total = total + parts_ref[i]
    total = total * factor
    for q in range(4):
        classed[4 * q : 4 * q + 4, :] = turn(total, -32 * q)
    sums = classed[:, 0:OUTS]
    f, h1, h2 = f_ref[...], h1_ref[...], h2_ref[...]
    two_grad = dot(sums, w3_ref[...].astype(F32), ((1,), (0,)), HIGHEST) * (1.0 - h2 * h2)
    one_grad = dot(two_grad, w2_ref[...].astype(F32), ((1,), (1,)), HIGHEST) * (1.0 - h1 * h1)
    feature_grad = dot(one_grad, w1_ref[...].astype(F32), ((1,), (1,)), HIGHEST)
    three_ref[...] = dot(sums, h2, ((0,), (0,)), HIGHEST)
    two_ref[...] = dot(h1, two_grad, ((0,), (0,)), HIGHEST)
    one_ref[...] = dot(f, one_grad, ((0,), (0,)), HIGHEST)
    embed_ref[...] = feature_grad
    scale = scale_ref[...].astype(F32) * (1.0 / 64.0)
    time_ref[...] = scale[0] * jnp.sum(feature_grad, axis=0)


def shift(x, axis, step):
    size = lax.axis_size(axis)
    pairs = [(i, i + step) for i in range(size) if 0 <= i + step < size]
    return lax.ppermute(x, axis, pairs)


def spread(x, axis, groups=None):
    size = lax.axis_size(axis) if groups is None else len(groups[0])
    copies = jnp.broadcast_to(x[None], (size,) + x.shape)
    return lax.all_to_all(copies, axis, 0, 0, tiled=True, axis_index_groups=groups)


def body(classes, check_index, snapshot, payoff, sensitivity, embed, time_vec, w_one, w_two, w_three):
    sd = jax.ShapeDtypeStruct
    tile = sd((GOALS, ROWS, COLS), BF16)
    marked = (classes + 1).astype(BF16)[None]
    everything = jnp.concatenate([snapshot, payoff, sensitivity, marked], axis=0)
    to_down, to_up = vmem_call(edge_kernel, (tile, tile), [pltpu.VMEM((ROWS, COLS), F32)] * 2)(everything)
    up = shift(to_down, "row", 1)
    down = shift(to_up, "row", -1)

    scale = jnp.broadcast_to(check_index.reshape(1, 1), (1, 64))
    layer = sd((CLASSES, 64), F32)
    square = sd((64, 64), BF16)
    table, feature, one, two, scale, w_one, w_two, w_three = vmem_call(
        table_kernel,
        (sd((72, COLS), F32), layer, layer, layer, sd((1, 64), jnp.int32), square, square, sd((OUTS, 64), BF16)),
        [pltpu.VMEM((32, COLS), F32), pltpu.VMEM((CLASSES, 64), BF16), pltpu.VMEM((1, 64), BF16),
         pltpu.SemaphoreType.DMA((6,))],
        source=pltpu.HBM,
    )(scale, embed, time_vec.reshape(1, -1), w_one, w_two, w_three.T)

    plane = pltpu.VMEM((EXT, COLS), F32)
    edge = sd((OCT + 1, 32, COLS), BF16)
    ext = sd((GOALS, EXT, COLS), F32)
    to_right, to_left, val, rew, sen, cls = vmem_call(
        strip_kernel, (edge, edge, ext, ext, ext, sd((EXT, COLS), F32))
    )(everything, up, down, table)
    left = shift(to_right, "col", 1)
    right = shift(to_left, "col", -1)

    strip = pltpu.VMEM((OCT, EXT, COLS), F32)

    def many(*shape):
        return pltpu.VMEM(shape + (COLS,), F32)

    n = ACTIONS * POINTS
    chance, bonus, mask, slope = vmem_call(
        map_kernel,
        (sd((n, EXT, COLS), F32), sd((ACTIONS, EXT, COLS), F32), sd((EXT, COLS), F32), sd((n, ROWS, COLS), F32)),
    )(cls, table)
    snap, pay, sums = vmem_call(
        main_kernel,
        (tile, tile, sd((4, COLS), F32)),
        [
            many(ITERS - 1, GOALS, EXT), many(ITERS, OCT, EXT), strip, strip, plane,
            many(n, EXT), many(ACTIONS, EXT), plane,
            many(ITERS, ACTIONS, GOALS, EXT), many(ITERS, ACTIONS, OCT, EXT),
            many(ITERS, GOALS, EXT), many(ITERS, GOALS, EXT),
            many(2, POINTS, GOALS, EXT), many(2, POINTS, OCT, EXT), many(GOALS, EXT),
            many(OUTS, ROWS), many(GOALS, ROWS), many(GOALS, ROWS),
        ],
    )(val, rew, sen, cls, chance, bonus, mask, slope, left, right, table)

    rows, cols = lax.axis_size("row"), lax.axis_size("col")
    near = [[r * cols + c + i for r in range(rows) for i in range(2)] for c in range(0, cols, 2)]
    along = [list(range(i, cols, 2)) for i in range(2)]
    sums = jnp.sum(spread(sums, ("row", "col"), near), axis=0)
    parts = spread(sums, "col", along)
    factor = 1.0 / math.sqrt(ROWS * lax.axis_size("row") * COLS * lax.axis_size("col"))

    def last(*refs):
        last_kernel(*refs, factor=factor)

    grads = vmem_call(
        last, (layer, sd((64,), F32), sd((64, 64), F32), sd((64, 64), F32), sd((OUTS, 64), F32)),
        [pltpu.VMEM((CLASSES, COLS), F32)],
    )(parts, scale, feature, one, two, w_one, w_two, w_three)
    return (snap, pay, grads[0], grads[1], grads[2], grads[3], grads[4].T)


def solution(mesh):
    tiled = P(None, "row", "col")
    return jax.shard_map(
        body,
        mesh=mesh,
        in_specs=(P("row", "col"), P(), tiled, tiled, tiled, P(), P(), P(), P(), P()),
        out_specs=(tiled, tiled, P(), P(), P(), P(), P()),
        check_vma=False,
    )
```

```python
import math

import jax
import jax.numpy as jnp
from jax import lax
from jax.experimental import pallas as pl
from jax.experimental.pallas import tpu as pltpu
from jax.sharding import PartitionSpec as P

ITERS = 3
ACTIONS = 4
POINTS = 5
OUTS = 24
GOALS = 24
CLASSES = 16
ROWS = 16
COLS = 128
DECAY = 0.9
SLACK = 0.05
VH, RH, FH = 6, 5, 3
TOP = 16
EXT = 48
GROUP = 16
OCT = GOALS // 8
HIGHEST = lax.Precision.HIGHEST
F32 = jnp.float32
BF16 = jnp.bfloat16


def vmem_call(kernel, out_shape, scratch=(), limit=40 * 1024 * 1024, source=pltpu.VMEM):
    whole = pl.BlockSpec(memory_space=pltpu.VMEM)
    given = pl.BlockSpec(memory_space=source)
    return lambda *args: pl.pallas_call(
        kernel,
        out_shape=out_shape,
        in_specs=[given] * len(args),
        out_specs=jax.tree.map(lambda _: whole, out_shape),
        scratch_shapes=list(scratch),
        compiler_params=pltpu.CompilerParams(vmem_limit_bytes=limit),
    )(*args)


def fetch(pairs, sems):
    copies = [pltpu.make_async_copy(a, b, sems.at[i]) for i, (a, b) in enumerate(pairs)]
    for copy in copies:
        copy.start()
    for copy in copies:
        copy.wait()


def lane_iota(shape):
    return lax.broadcasted_iota(jnp.int32, shape, len(shape) - 1)


def turn(x, shift):
    shift = shift % COLS
    return x if shift == 0 else pltpu.roll(x, shift, 1)


def dot(a, b, dims, precision=None):
    return lax.dot_general(a, b, (dims, ((), ())), precision=precision, preferred_element_type=F32)


def table_kernel(scale_hbm, embed_hbm, time_hbm, w1_hbm, w2_hbm, w3_hbm, tab_ref, f_ref, h1_ref, h2_ref,
                 scale_ref, w1_ref, w2_ref, w3_ref, raw, embed_ref, time_ref, sems):
    fetch(((scale_hbm, scale_ref), (embed_hbm, embed_ref), (time_hbm, time_ref),
           (w1_hbm, w1_ref), (w2_hbm, w2_ref), (w3_hbm, w3_ref)), sems)
    scale = scale_ref[...].astype(F32) * (1.0 / 64.0)
    feature = (embed_ref[...].astype(F32) + scale * time_ref[...].astype(F32)).astype(BF16)
    one = jnp.tanh(dot(feature, w1_ref[...], ((1,), (0,)))).astype(BF16)
    two = jnp.tanh(dot(one, w2_ref[...], ((1,), (0,)))).astype(BF16)
    f_ref[...] = feature.astype(F32)
    h1_ref[...] = one.astype(F32)
    h2_ref[...] = two.astype(F32)
    logits = dot(w3_ref[...], two, ((1,), (1,)))
    raw[...] = jnp.zeros_like(raw)
    tab_ref[...] = jnp.zeros_like(tab_ref)
    for a in range(ACTIONS):
        raw[8 * a : 8 * a + POINTS, 0:CLASSES] = logits[a * POINTS : (a + 1) * POINTS]
    valid = lax.broadcasted_iota(jnp.int32, (8, COLS), 0) < POINTS
    for a in range(ACTIONS):
        x = raw[8 * a : 8 * a + 8, :]
        weight = jnp.maximum(x, 0.0) + jnp.log(1.0 + jnp.exp(-jnp.abs(x))) + SLACK
        total = jnp.sum(jnp.where(valid, weight, 0.0), axis=0, keepdims=True)
        tab_ref[16 * a : 16 * a + 8, :] = DECAY * weight / total
        tab_ref[16 * a + 8 : 16 * a + 16, :] = 1.0 / ((1.0 + jnp.exp(-x)) * total)
    tab_ref[64:68, 0:CLASSES] = logits[ACTIONS * POINTS :]


def chance_row(a, k):
    return 16 * a + k


def slope_row(a, k):
    return 16 * a + 8 + k


def bonus_row(a):
    return 64 + a


def edge_kernel(all_ref, to_down, to_up, low, high):
    low[...] = jnp.zeros_like(low)
    high[...] = jnp.zeros_like(high)
    marked = all_ref[3 * GOALS].astype(F32)
    for g in range(GOALS):
        v, r, s = [all_ref[i * GOALS + g].astype(F32) for i in range(3)]
        low[0:6, :], low[6:11, :], low[11:14, :] = v[ROWS - VH :], r[ROWS - RH :], s[ROWS - FH :]
        high[0:6, :], high[6:11, :], high[11:14, :] = v[0:VH], r[0:RH], s[0:FH]
        if g < RH:
            low[14:15, :], high[14:15, :] = marked[ROWS - RH + g : ROWS - RH + g + 1], marked[g : g + 1]
        to_down[g] = low[...].astype(BF16)
        to_up[g] = high[...].astype(BF16)


def fill_rows(dst, g, up, mid, down, n):
    dst[g, TOP - n : TOP, :] = up
    dst[g, TOP : TOP + ROWS, :] = mid
    dst[g, TOP + ROWS : TOP + ROWS + n, :] = down


def extend_rows(all_ref, up_ref, down_ref, val, rew, sen, cls):
    def one(g, carry):
        up = up_ref[g].astype(F32)
        down = down_ref[g].astype(F32)
        fill_rows(val, g, up[0:6], all_ref[g].astype(F32), down[0:6], VH)
        fill_rows(rew, g, up[6:11], all_ref[GOALS + g].astype(F32), down[6:11], RH)
        fill_rows(sen, g, up[11:14], all_ref[2 * GOALS + g].astype(F32), down[11:14], FH)
        return carry

    lax.fori_loop(0, GOALS, one, 0, unroll=4)
    cls[...] = jnp.zeros_like(cls)
    cls[TOP : TOP + ROWS, :] = all_ref[3 * GOALS].astype(F32)
    for i in range(RH):
        cls[TOP - RH + i : TOP - RH + i + 1, :] = up_ref[i, 14:15, :].astype(F32)
        cls[TOP + ROWS + i : TOP + ROWS + i + 1, :] = down_ref[i, 14:15, :].astype(F32)


def strip_kernel(all_ref, up_ref, down_ref, tab_ref, to_right, to_left, val, rew, sen, cls):
    extend_rows(all_ref, up_ref, down_ref, val, rew, sen, cls)
    group_lane = lane_iota((8, COLS)) % GROUP
    group_at = lane_iota((8, COLS)) // GROUP

    def octet(o, carry):
        for j in range(4):
            rows = slice(8 + 8 * j, 16 + 8 * j)
            right = jnp.zeros((8, COLS), F32)
            left = jnp.zeros((8, COLS), F32)
            for q in range(8):
                p = GROUP * q
                v, r, s = val[o * 8 + q, rows, :], rew[o * 8 + q, rows, :], sen[o * 8 + q, rows, :]
                here = group_at == q
                part = jnp.where(group_lane < 11, turn(r, p + 11), turn(s, p + 14))
                right = jnp.where(here, jnp.where(group_lane < 6, turn(v, p + 6), part), right)
                part = jnp.where(group_lane < 11, turn(r, p + 6), turn(s, p + 11))
                left = jnp.where(here, jnp.where(group_lane < 6, turn(v, p), part), left)
            to_right[o, 8 * j : 8 * j + 8, :] = right.astype(to_right.dtype)
            to_left[o, 8 * j : 8 * j + 8, :] = left.astype(to_left.dtype)
        return carry

    lax.fori_loop(0, OCT, octet, 0)
    for j in range(4):
        c = cls[8 + 8 * j : 16 + 8 * j, :]
        right = jnp.zeros((8, COLS), F32)
        left = jnp.zeros((8, COLS), F32)
        for q in range(8):
            here = group_at == q
            right = jnp.where(here, turn(c, GROUP * q + 6), right)
            left = jnp.where(here, turn(c, GROUP * q), left)
        to_right[OCT, 8 * j : 8 * j + 8, :] = right.astype(to_right.dtype)
        to_left[OCT, 8 * j : 8 * j + 8, :] = left.astype(to_left.dtype)


def look_up(base, cls, tab_ref, chance, bonus, mask, slope=None):
    at = slice(base, base + 8)
    number = cls[at, :].astype(jnp.int32)
    inside = number > 0
    which = jnp.maximum(number - 1, 0)
    mask[at, :] = inside.astype(F32)

    def look(row):
        table = jnp.broadcast_to(tab_ref[row : row + 1, :], (8, COLS))
        return jnp.where(inside, jnp.take_along_axis(table, which, axis=1), 0.0)

    for a in range(ACTIONS):
        for k in range(POINTS):
            chance[a * POINTS + k, at, :] = look(chance_row(a, k))
            if slope is not None:
                slope[a * POINTS + k, base - TOP : base - TOP + 8, :] = look(slope_row(a, k))
        bonus[a, at, :] = look(bonus_row(a))


def map_kernel(cls, tab_ref, chance, bonus, mask, slope):
    for j in range(4):
        look_up(8 + 8 * j, cls, tab_ref, chance, bonus, mask, slope if j in (1, 2) else None)


def main_kernel(val0, rew, sen, cls, chance, bonus, mask, slope, lb_ref, rb_ref, tab_ref,
                snap_ref, pay_ref, sums_ref,
                later, sval, srew, ssen, scls, schance, sbonus, smask,
                soft, ssoft, lshift, rshift, push, spush, adjoint, cgrad, paysum, packed):
    val = [val0, later.at[0], later.at[1]]
    lane = lane_iota((8, COLS))
    glane = lane % GROUP
    inner = glane < 6
    first, last = lane == 0, lane == COLS - 1
    strip_first, strip_last = glane == 5, glane == 6
    for o in range(OCT + 1):
        for j in range(4):
            left = lb_ref[o, 8 * j : 8 * j + 8, :].astype(F32)
            right = rb_ref[o, 8 * j : 8 * j + 8, :].astype(F32)
            at = slice(8 + 8 * j, 16 + 8 * j)
            outer = jnp.where(inner, left, turn(right, 6))
            if o == OCT:
                scls[at, :] = jnp.where(glane < 12, outer, 0.0)
            else:
                sval[0, o, at, :] = outer
                srew[o, at, :] = jnp.where(inner, turn(left, -5), right)
                ssen[o, at, :] = jnp.where(inner, turn(left, -8), turn(right, -5))
    for j in range(4):
        look_up(8 + 8 * j, scls, tab_ref, schance, sbonus, smask)

    def where_tile(start):
        base = TOP + start
        return slice(base, base + 8), slice(base - 1, base + 7), slice(base + 1, base + 9)

    def soft_step(near, reward, ch, bo, keep_value):
        q = []
        for a in range(ACTIONS):
            total = reward + bo[a]
            for k in range(POINTS):
                total = total + ch[a * POINTS + k] * near[k]
            q.append(total)
        highest = jnp.maximum(jnp.maximum(q[0], q[1]), jnp.maximum(q[2], q[3]))
        e = [jnp.exp(x - highest) for x in q]
        total = (e[0] + e[1]) + (e[2] + e[3])
        inverse = 1.0 / total
        value = highest + jnp.log(total) if keep_value else None
        return [x * inverse for x in e], value

    for t in range(ITERS):
        keep = t < ITERS - 1

        def forward(o, start, t=t, keep=keep):
            rows, above, below = where_tile(start)
            ch = [chance[n, rows, :] for n in range(ACTIONS * POINTS)]
            bo = [bonus[a, rows, :] for a in range(ACTIONS)]
            sv = sval[t, o, rows, :]
            edge = jnp.zeros((8, COLS), F32)
            for q in range(8):
                p, g = GROUP * q, o * 8 + q
                x = val[t][g, rows, :]
                fill = turn(sv, -(p + 6))
                toleft = turn(jnp.where(last, fill, x), 1)
                toright = turn(jnp.where(first, fill, x), -1)
                edge = jnp.where((lane == p + 5) | (lane == p + 6), turn(x, p + 6), edge)
                lshift[t, g, rows, :] = toleft
                rshift[t, g, rows, :] = toright
                near = [x, val[t][g, above, :], val[t][g, below, :], toleft, toright]
                probs, value = soft_step(near, rew[g, rows, :], ch, bo, keep)
                for a in range(ACTIONS):
                    soft[t, a, g, rows, :] = probs[a]
                if keep:
                    val[t + 1][g, rows, :] = value * mask[rows, :]
            near = [sv, sval[t, o, above, :], sval[t, o, below, :],
                    turn(jnp.where(strip_first, edge, sv), 1), turn(jnp.where(strip_last, edge, sv), -1)]
            ch = [schance[n, rows, :] for n in range(ACTIONS * POINTS)]
            bo = [sbonus[a, rows, :] for a in range(ACTIONS)]
            probs, value = soft_step(near, srew[o, rows, :], ch, bo, keep)
            for a in range(ACTIONS):
                ssoft[t, a, o, rows, :] = probs[a]
            if keep:
                sval[t + 1, o, rows, :] = value * smask[rows, :]

        starts = (-6, 2, 10, 18) if t == 0 else (-4, 4, 12)

        def forward_all(o, carry, forward=forward, starts=starts):
            for start in starts:
                forward(o, start)
            return carry

        lax.fori_loop(0, OCT, forward_all, 0)

    cgrad[...] = jnp.zeros_like(cgrad)
    paysum[...] = jnp.zeros_like(paysum)

    def gather(o, rows, above, below, old):
        s3, s4 = spush[old, 3, o, rows, :], spush[old, 4, o, rows, :]
        both = jnp.where(strip_last, s3, s4)
        edge = jnp.zeros((8, COLS), F32)
        out = []
        for q in range(8):
            p, g = GROUP * q, o * 8 + q
            p3, p4 = push[old, 3, g, rows, :], push[old, 4, g, rows, :]
            fill = turn(both, -(p + 6))
            from_right = turn(jnp.where(first, fill, p3), -1)
            from_left = turn(jnp.where(last, fill, p4), 1)
            edge = jnp.where((lane == p + 5) | (lane == p + 6), turn(jnp.where(first, p3, p4), p + 6), edge)
            out.append(push[old, 0, g, rows, :] + push[old, 1, g, below, :] + push[old, 2, g, above, :]
                       + from_right + from_left)
        strip = (spush[old, 0, o, rows, :] + spush[old, 1, o, below, :] + spush[old, 2, o, above, :]
                 + turn(jnp.where(strip_last, edge, s3), -1) + turn(jnp.where(strip_first, edge, s4), 1))
        return out, strip

    for t in reversed(range(ITERS)):
        new, old = t % 2, (t + 1) % 2

        def spread_out(o, start, t=t, new=new, old=old):
            rows, above, below = where_tile(start)
            if t == ITERS - 1:
                adj = [sen[o * 8 + q, rows, :] for q in range(8)]
                strip = ssen[o, rows, :]
            else:
                adj, strip = gather(o, rows, above, below, old)
                for q in range(8):
                    adjoint[o * 8 + q, rows, :] = adj[q]
            for q in range(8):
                g = o * 8 + q
                grads = [adj[q] * soft[t, a, g, rows, :] for a in range(ACTIONS)]
                for k in range(POINTS):
                    total = grads[0] * chance[k, rows, :]
                    for a in range(1, ACTIONS):
                        total = total + grads[a] * chance[a * POINTS + k, rows, :]
                    push[new, k, g, rows, :] = total
            grads = [strip * ssoft[t, a, o, rows, :] for a in range(ACTIONS)]
            for k in range(POINTS):
                total = grads[0] * schance[k, rows, :]
                for a in range(1, ACTIONS):
                    total = total + grads[a] * schance[a * POINTS + k, rows, :]
                spush[new, k, o, rows, :] = total

        def collect(o, start, t=t):
            rows, above, below = where_tile(start)
            source = sen if t == ITERS - 1 else adjoint
            adj = [source[o * 8 + q, rows, :] for q in range(8)]
            at = slice(start, start + 8)
            for q in range(8):
                g = o * 8 + q
                grads = [adj[q] * soft[t, a, g, rows, :] for a in range(ACTIONS)]
                paysum[g, at, :] += (grads[0] + grads[1]) + (grads[2] + grads[3])
            for a in range(ACTIONS):
                sums = [cgrad[a * POINTS + k, at, :] for k in range(POINTS)]
                total = cgrad[ACTIONS * POINTS + a, at, :]
                for q in range(8):
                    g = o * 8 + q
                    grad = adj[q] * soft[t, a, g, rows, :]
                    total = total + grad
                    near = [val[t][g, rows, :], val[t][g, above, :], val[t][g, below, :],
                            lshift[t, g, rows, :], rshift[t, g, rows, :]]
                    sums = [x + grad * y for x, y in zip(sums, near)]
                for k in range(POINTS):
                    cgrad[a * POINTS + k, at, :] = sums[k]
                cgrad[ACTIONS * POINTS + a, at, :] = total

        def backward_all(o, carry, spread_out=spread_out, collect=collect):
            for start in (-4, 4, 12):
                spread_out(o, start)
            for start in (0, 8):
                collect(o, start)
            return carry

        lax.fori_loop(0, OCT, backward_all, 0)

    def finish(o, carry):
        for start in (0, 8):
            rows, above, below = where_tile(start)
            adj = gather(o, rows, above, below, 0)[0]
            for q in range(8):
                packed[o * 8 + q, start : start + 8, :] = adj[q]
        return carry

    lax.fori_loop(0, OCT, finish, 0)
    snap_ref[...] = packed[...].astype(BF16)
    pay_ref[...] = paysum[...].astype(BF16)
    for j in range(2):
        at = slice(8 * j, 8 * j + 8)
        rows = slice(TOP + 8 * j, TOP + 8 * j + 8)
        for a in range(ACTIONS):
            grads = [cgrad[a * POINTS + k, at, :] for k in range(POINTS)]
            weighted = grads[0] * chance[a * POINTS, rows, :]
            for k in range(1, POINTS):
                weighted = weighted + grads[k] * chance[a * POINTS + k, rows, :]
            for k in range(POINTS):
                cgrad[a * POINTS + k, at, :] = (DECAY * grads[k] - weighted) * slope[a * POINTS + k, at, :]
    number = lax.broadcasted_iota(jnp.int32, (CLASSES, COLS), 0)
    total = jnp.zeros((CLASSES, OUTS), F32)
    which = cls[TOP : TOP + ROWS, :].astype(jnp.int32) - 1
    for i in range(ROWS):
        one_hot = (number == which[i : i + 1]).astype(BF16)
        total = total + dot(one_hot, cgrad[:, i, :].astype(BF16), ((1,), (1,)))
    packed[0, :, :] = jnp.zeros((ROWS, COLS), F32)
    packed[0, 0:CLASSES, 0:OUTS] = total
    parts = [packed[0, 4 * q : 4 * q + 4, :] for q in range(4)]
    sums_ref[...] = (parts[0] + turn(parts[1], 32)) + (turn(parts[2], 64) + turn(parts[3], 96))


def last_kernel(parts_ref, scale_ref, f_ref, h1_ref, h2_ref, w1_ref, w2_ref, w3_ref,
                embed_ref, time_ref, one_ref, two_ref, three_ref, classed, *, factor):
    total = parts_ref[0]
    for i in range(1, parts_ref.shape[0]):
        total = total + parts_ref[i]
    total = total * factor
    for q in range(4):
        classed[4 * q : 4 * q + 4, :] = turn(total, -32 * q)
    sums = classed[:, 0:OUTS]
    f, h1, h2 = f_ref[...], h1_ref[...], h2_ref[...]
    two_grad = dot(sums, w3_ref[...].astype(F32), ((1,), (0,)), HIGHEST) * (1.0 - h2 * h2)
    one_grad = dot(two_grad, w2_ref[...].astype(F32), ((1,), (1,)), HIGHEST) * (1.0 - h1 * h1)
    feature_grad = dot(one_grad, w1_ref[...].astype(F32), ((1,), (1,)), HIGHEST)
    three_ref[...] = dot(sums, h2, ((0,), (0,)), HIGHEST)
    two_ref[...] = dot(h1, two_grad, ((0,), (0,)), HIGHEST)
    one_ref[...] = dot(f, one_grad, ((0,), (0,)), HIGHEST)
    embed_ref[...] = feature_grad
    scale = scale_ref[...].astype(F32) * (1.0 / 64.0)
    time_ref[...] = scale[0] * jnp.sum(feature_grad, axis=0)


def shift(x, axis, step):
    size = lax.axis_size(axis)
    pairs = [(i, i + step) for i in range(size) if 0 <= i + step < size]
    return lax.ppermute(x, axis, pairs)


def spread(x, axis, groups=None):
    size = lax.axis_size(axis) if groups is None else len(groups[0])
    copies = jnp.broadcast_to(x[None], (size,) + x.shape)
    return lax.all_to_all(copies, axis, 0, 0, tiled=True, axis_index_groups=groups)


def body(classes, check_index, snapshot, payoff, sensitivity, embed, time_vec, w_one, w_two, w_three):
    sd = jax.ShapeDtypeStruct
    tile = sd((GOALS, ROWS, COLS), BF16)
    marked = (classes + 1).astype(BF16)[None]
    everything = jnp.concatenate([snapshot, payoff, sensitivity, marked], axis=0)
    to_down, to_up = vmem_call(edge_kernel, (tile, tile), [pltpu.VMEM((ROWS, COLS), F32)] * 2)(everything)
    up = shift(to_down, "row", 1)
    down = shift(to_up, "row", -1)

    scale = jnp.broadcast_to(check_index.reshape(1, 1), (1, 64))
    layer = sd((CLASSES, 64), F32)
    square = sd((64, 64), BF16)
    table, feature, one, two, scale, w_one, w_two, w_three = vmem_call(
        table_kernel,
        (sd((72, COLS), F32), layer, layer, layer, sd((1, 64), jnp.int32), square, square, sd((OUTS, 64), BF16)),
        [pltpu.VMEM((32, COLS), F32), pltpu.VMEM((CLASSES, 64), BF16), pltpu.VMEM((1, 64), BF16),
         pltpu.SemaphoreType.DMA((6,))],
        source=pltpu.HBM,
    )(scale, embed, time_vec.reshape(1, -1), w_one, w_two, w_three.T)

    plane = pltpu.VMEM((EXT, COLS), F32)
    edge = sd((OCT + 1, 32, COLS), BF16)
    ext = sd((GOALS, EXT, COLS), F32)
    to_right, to_left, val, rew, sen, cls = vmem_call(
        strip_kernel, (edge, edge, ext, ext, ext, sd((EXT, COLS), F32))
    )(everything, up, down, table)
    left = shift(to_right, "col", 1)
    right = shift(to_left, "col", -1)

    strip = pltpu.VMEM((OCT, EXT, COLS), F32)

    def many(*shape):
        return pltpu.VMEM(shape + (COLS,), F32)

    n = ACTIONS * POINTS
    chance, bonus, mask, slope = vmem_call(
        map_kernel,
        (sd((n, EXT, COLS), F32), sd((ACTIONS, EXT, COLS), F32), sd((EXT, COLS), F32), sd((n, ROWS, COLS), F32)),
    )(cls, table)
    snap, pay, sums = vmem_call(
        main_kernel,
        (tile, tile, sd((4, COLS), F32)),
        [
            many(ITERS - 1, GOALS, EXT), many(ITERS, OCT, EXT), strip, strip, plane,
            many(n, EXT), many(ACTIONS, EXT), plane,
            many(ITERS, ACTIONS, GOALS, EXT), many(ITERS, ACTIONS, OCT, EXT),
            many(ITERS, GOALS, EXT), many(ITERS, GOALS, EXT),
            many(2, POINTS, GOALS, EXT), many(2, POINTS, OCT, EXT), many(GOALS, EXT),
            many(OUTS, ROWS), many(GOALS, ROWS), many(GOALS, ROWS),
        ],
    )(val, rew, sen, cls, chance, bonus, mask, slope, left, right, table)

    rows, cols = lax.axis_size("row"), lax.axis_size("col")
    near = [[r * cols + c + i for r in range(rows) for i in range(2)] for c in range(0, cols, 2)]
    along = [list(range(i, cols, 2)) for i in range(2)]
    sums = jnp.sum(spread(sums, "col", along), axis=0)
    parts = spread(sums, ("row", "col"), near)
    factor = 1.0 / math.sqrt(ROWS * lax.axis_size("row") * COLS * lax.axis_size("col"))

    def last(*refs):
        last_kernel(*refs, factor=factor)

    grads = vmem_call(
        last, (layer, sd((64,), F32), sd((64, 64), F32), sd((64, 64), F32), sd((OUTS, 64), F32)),
        [pltpu.VMEM((CLASSES, COLS), F32)],
    )(parts, scale, feature, one, two, w_one, w_two, w_three)
    return (snap, pay, grads[0], grads[1], grads[2], grads[3], grads[4].T)


def solution(mesh):
    tiled = P(None, "row", "col")
    return jax.shard_map(
        body,
        mesh=mesh,
        in_specs=(P("row", "col"), P(), tiled, tiled, tiled, P(), P(), P(), P(), P()),
        out_specs=(tiled, tiled, P(), P(), P(), P(), P()),
        check_vma=False,
    )
```

```python
import math

import jax
import jax.numpy as jnp
from jax import lax
from jax.experimental import pallas as pl
from jax.experimental.pallas import tpu as pltpu
from jax.sharding import PartitionSpec as P

ITERS = 3
ACTIONS = 4
POINTS = 5
OUTS = 24
GOALS = 24
CLASSES = 16
ROWS = 16
COLS = 128
DECAY = 0.9
SLACK = 0.05
VH, RH, FH = 6, 5, 3
TOP = 16
EXT = 48
GROUP = 16
OCT = GOALS // 8
HIGHEST = lax.Precision.HIGHEST
F32 = jnp.float32
BF16 = jnp.bfloat16


def vmem_call(kernel, out_shape, scratch=(), limit=40 * 1024 * 1024, source=pltpu.VMEM):
    whole = pl.BlockSpec(memory_space=pltpu.VMEM)
    given = pl.BlockSpec(memory_space=source)
    return lambda *args: pl.pallas_call(
        kernel,
        out_shape=out_shape,
        in_specs=[given] * len(args),
        out_specs=jax.tree.map(lambda _: whole, out_shape),
        scratch_shapes=list(scratch),
        compiler_params=pltpu.CompilerParams(vmem_limit_bytes=limit),
    )(*args)


def fetch(pairs, sems):
    copies = [pltpu.make_async_copy(a, b, sems.at[i]) for i, (a, b) in enumerate(pairs)]
    for copy in copies:
        copy.start()
    for copy in copies:
        copy.wait()


def lane_iota(shape):
    return lax.broadcasted_iota(jnp.int32, shape, len(shape) - 1)


def turn(x, shift):
    shift = shift % COLS
    return x if shift == 0 else pltpu.roll(x, shift, 1)


def dot(a, b, dims, precision=None):
    return lax.dot_general(a, b, (dims, ((), ())), precision=precision, preferred_element_type=F32)


def split_dot(x, y, dims):
    total = None
    for _ in range(3):
        part = x.astype(BF16)
        x = x - part.astype(F32)
        one = dot(part, y, dims)
        total = one if total is None else total + one
    return total


def table_kernel(scale_hbm, embed_hbm, time_hbm, w1_hbm, w2_hbm, w3_hbm, tab_ref, f_ref, h1_ref, h2_ref,
                 scale_ref, w1_ref, w2_ref, w3_ref, raw, embed_ref, time_ref, sems):
    fetch(((scale_hbm, scale_ref), (embed_hbm, embed_ref), (time_hbm, time_ref),
           (w1_hbm, w1_ref), (w2_hbm, w2_ref), (w3_hbm, w3_ref)), sems)
    scale = scale_ref[...].astype(F32) * (1.0 / 64.0)
    feature = (embed_ref[...].astype(F32) + scale * time_ref[...].astype(F32)).astype(BF16)
    one = jnp.tanh(dot(feature, w1_ref[...], ((1,), (0,)))).astype(BF16)
    two = jnp.tanh(dot(one, w2_ref[...], ((1,), (0,)))).astype(BF16)
    f_ref[...] = feature.astype(F32)
    h1_ref[...] = one.astype(F32)
    h2_ref[...] = two.astype(F32)
    logits = dot(w3_ref[...], two, ((1,), (1,)))
    raw[...] = jnp.zeros_like(raw)
    tab_ref[...] = jnp.zeros_like(tab_ref)
    for a in range(ACTIONS):
        raw[8 * a : 8 * a + POINTS, 0:CLASSES] = logits[a * POINTS : (a + 1) * POINTS]
    valid = lax.broadcasted_iota(jnp.int32, (8, COLS), 0) < POINTS
    for a in range(ACTIONS):
        x = raw[8 * a : 8 * a + 8, :]
        weight = jnp.maximum(x, 0.0) + jnp.log(1.0 + jnp.exp(-jnp.abs(x))) + SLACK
        total = jnp.sum(jnp.where(valid, weight, 0.0), axis=0, keepdims=True)
        tab_ref[16 * a : 16 * a + 8, :] = DECAY * weight / total
        tab_ref[16 * a + 8 : 16 * a + 16, :] = 1.0 / ((1.0 + jnp.exp(-x)) * total)
    tab_ref[64:68, 0:CLASSES] = logits[ACTIONS * POINTS :]


def chance_row(a, k):
    return 16 * a + k


def slope_row(a, k):
    return 16 * a + 8 + k


def bonus_row(a):
    return 64 + a


def edge_kernel(all_ref, to_down, to_up, low, high):
    low[...] = jnp.zeros_like(low)
    high[...] = jnp.zeros_like(high)
    marked = all_ref[3 * GOALS].astype(F32)
    for g in range(GOALS):
        v, r, s = [all_ref[i * GOALS + g].astype(F32) for i in range(3)]
        low[0:6, :], low[6:11, :], low[11:14, :] = v[ROWS - VH :], r[ROWS - RH :], s[ROWS - FH :]
        high[0:6, :], high[6:11, :], high[11:14, :] = v[0:VH], r[0:RH], s[0:FH]
        if g < RH:
            low[14:15, :], high[14:15, :] = marked[ROWS - RH + g : ROWS - RH + g + 1], marked[g : g + 1]
        to_down[g] = low[...].astype(BF16)
        to_up[g] = high[...].astype(BF16)


def fill_rows(dst, g, up, mid, down, n):
    dst[g, TOP - n : TOP, :] = up
    dst[g, TOP : TOP + ROWS, :] = mid
    dst[g, TOP + ROWS : TOP + ROWS + n, :] = down


def extend_rows(all_ref, up_ref, down_ref, val, rew, sen, cls):
    def one(g, carry):
        up = up_ref[g].astype(F32)
        down = down_ref[g].astype(F32)
        fill_rows(val, g, up[0:6], all_ref[g].astype(F32), down[0:6], VH)
        fill_rows(rew, g, up[6:11], all_ref[GOALS + g].astype(F32), down[6:11], RH)
        fill_rows(sen, g, up[11:14], all_ref[2 * GOALS + g].astype(F32), down[11:14], FH)
        return carry

    lax.fori_loop(0, GOALS, one, 0, unroll=4)
    cls[...] = jnp.zeros_like(cls)
    cls[TOP : TOP + ROWS, :] = all_ref[3 * GOALS].astype(F32)
    for i in range(RH):
        cls[TOP - RH + i : TOP - RH + i + 1, :] = up_ref[i, 14:15, :].astype(F32)
        cls[TOP + ROWS + i : TOP + ROWS + i + 1, :] = down_ref[i, 14:15, :].astype(F32)


def strip_kernel(all_ref, up_ref, down_ref, tab_ref, to_right, to_left, val, rew, sen, cls):
    extend_rows(all_ref, up_ref, down_ref, val, rew, sen, cls)
    group_lane = lane_iota((8, COLS)) % GROUP
    group_at = lane_iota((8, COLS)) // GROUP

    def octet(o, carry):
        for j in range(4):
            rows = slice(8 + 8 * j, 16 + 8 * j)
            right = jnp.zeros((8, COLS), F32)
            left = jnp.zeros((8, COLS), F32)
            for q in range(8):
                p = GROUP * q
                v, r, s = val[o * 8 + q, rows, :], rew[o * 8 + q, rows, :], sen[o * 8 + q, rows, :]
                here = group_at == q
                part = jnp.where(group_lane < 11, turn(r, p + 11), turn(s, p + 14))
                right = jnp.where(here, jnp.where(group_lane < 6, turn(v, p + 6), part), right)
                part = jnp.where(group_lane < 11, turn(r, p + 6), turn(s, p + 11))
                left = jnp.where(here, jnp.where(group_lane < 6, turn(v, p), part), left)
            to_right[o, 8 * j : 8 * j + 8, :] = right.astype(to_right.dtype)
            to_left[o, 8 * j : 8 * j + 8, :] = left.astype(to_left.dtype)
        return carry

    lax.fori_loop(0, OCT, octet, 0)
    for j in range(4):
        c = cls[8 + 8 * j : 16 + 8 * j, :]
        right = jnp.zeros((8, COLS), F32)
        left = jnp.zeros((8, COLS), F32)
        for q in range(8):
            here = group_at == q
            right = jnp.where(here, turn(c, GROUP * q + 6), right)
            left = jnp.where(here, turn(c, GROUP * q), left)
        to_right[OCT, 8 * j : 8 * j + 8, :] = right.astype(to_right.dtype)
        to_left[OCT, 8 * j : 8 * j + 8, :] = left.astype(to_left.dtype)


def look_up(base, cls, tab_ref, chance, bonus, mask, slope=None):
    at = slice(base, base + 8)
    number = cls[at, :].astype(jnp.int32)
    inside = number > 0
    which = jnp.maximum(number - 1, 0)
    mask[at, :] = inside.astype(F32)

    def look(row):
        table = jnp.broadcast_to(tab_ref[row : row + 1, :], (8, COLS))
        return jnp.where(inside, jnp.take_along_axis(table, which, axis=1), 0.0)

    for a in range(ACTIONS):
        for k in range(POINTS):
            chance[a * POINTS + k, at, :] = look(chance_row(a, k))
            if slope is not None:
                slope[a * POINTS + k, base - TOP : base - TOP + 8, :] = look(slope_row(a, k))
        bonus[a, at, :] = look(bonus_row(a))


def map_kernel(cls, tab_ref, chance, bonus, mask, slope):
    for j in range(4):
        look_up(8 + 8 * j, cls, tab_ref, chance, bonus, mask, slope if j in (1, 2) else None)


def main_kernel(val0, rew, sen, cls, chance, bonus, mask, slope, lb_ref, rb_ref, tab_ref,
                snap_ref, pay_ref, sums_ref,
                later, sval, srew, ssen, scls, schance, sbonus, smask,
                soft, ssoft, lshift, rshift, push, spush, adjoint, cgrad, paysum, packed):
    val = [val0, later.at[0], later.at[1]]
    lane = lane_iota((8, COLS))
    glane = lane % GROUP
    inner = glane < 6
    first, last = lane == 0, lane == COLS - 1
    strip_first, strip_last = glane == 5, glane == 6
    for o in range(OCT + 1):
        for j in range(4):
            left = lb_ref[o, 8 * j : 8 * j + 8, :].astype(F32)
            right = rb_ref[o, 8 * j : 8 * j + 8, :].astype(F32)
            at = slice(8 + 8 * j, 16 + 8 * j)
            outer = jnp.where(inner, left, turn(right, 6))
            if o == OCT:
                scls[at, :] = jnp.where(glane < 12, outer, 0.0)
            else:
                sval[0, o, at, :] = outer
                srew[o, at, :] = jnp.where(inner, turn(left, -5), right)
                ssen[o, at, :] = jnp.where(inner, turn(left, -8), turn(right, -5))
    for j in range(4):
        look_up(8 + 8 * j, scls, tab_ref, schance, sbonus, smask)

    def where_tile(start):
        base = TOP + start
        return slice(base, base + 8), slice(base - 1, base + 7), slice(base + 1, base + 9)

    def soft_step(near, reward, ch, bo, keep_value):
        q = []
        for a in range(ACTIONS):
            total = reward + bo[a]
            for k in range(POINTS):
                total = total + ch[a * POINTS + k] * near[k]
            q.append(total)
        highest = jnp.maximum(jnp.maximum(q[0], q[1]), jnp.maximum(q[2], q[3]))
        e = [jnp.exp(x - highest) for x in q]
        total = (e[0] + e[1]) + (e[2] + e[3])
        inverse = 1.0 / total
        value = highest + jnp.log(total) if keep_value else None
        return [x * inverse for x in e], value

    for t in range(ITERS):
        keep = t < ITERS - 1

        def forward(o, start, t=t, keep=keep):
            rows, above, below = where_tile(start)
            ch = [chance[n, rows, :] for n in range(ACTIONS * POINTS)]
            bo = [bonus[a, rows, :] for a in range(ACTIONS)]
            sv = sval[t, o, rows, :]
            edge = jnp.zeros((8, COLS), F32)
            for q in range(8):
                p, g = GROUP * q, o * 8 + q
                x = val[t][g, rows, :]
                fill = turn(sv, -(p + 6))
                toleft = turn(jnp.where(last, fill, x), 1)
                toright = turn(jnp.where(first, fill, x), -1)
                edge = jnp.where((lane == p + 5) | (lane == p + 6), turn(x, p + 6), edge)
                lshift[t, g, rows, :] = toleft
                rshift[t, g, rows, :] = toright
                near = [x, val[t][g, above, :], val[t][g, below, :], toleft, toright]
                probs, value = soft_step(near, rew[g, rows, :], ch, bo, keep)
                for a in range(ACTIONS):
                    soft[t, a, g, rows, :] = probs[a]
                if keep:
                    val[t + 1][g, rows, :] = value * mask[rows, :]
            near = [sv, sval[t, o, above, :], sval[t, o, below, :],
                    turn(jnp.where(strip_first, edge, sv), 1), turn(jnp.where(strip_last, edge, sv), -1)]
            ch = [schance[n, rows, :] for n in range(ACTIONS * POINTS)]
            bo = [sbonus[a, rows, :] for a in range(ACTIONS)]
            probs, value = soft_step(near, srew[o, rows, :], ch, bo, keep)
            for a in range(ACTIONS):
                ssoft[t, a, o, rows, :] = probs[a]
            if keep:
                sval[t + 1, o, rows, :] = value * smask[rows, :]

        starts = (-6, 2, 10, 18) if t == 0 else (-4, 4, 12)

        def forward_all(o, carry, forward=forward, starts=starts):
            for start in starts:
                forward(o, start)
            return carry

        lax.fori_loop(0, OCT, forward_all, 0)

    cgrad[...] = jnp.zeros_like(cgrad)
    paysum[...] = jnp.zeros_like(paysum)

    def gather(o, rows, above, below, old):
        s3, s4 = spush[old, 3, o, rows, :], spush[old, 4, o, rows, :]
        both = jnp.where(strip_last, s3, s4)
        edge = jnp.zeros((8, COLS), F32)
        out = []
        for q in range(8):
            p, g = GROUP * q, o * 8 + q
            p3, p4 = push[old, 3, g, rows, :], push[old, 4, g, rows, :]
            fill = turn(both, -(p + 6))
            from_right = turn(jnp.where(first, fill, p3), -1)
            from_left = turn(jnp.where(last, fill, p4), 1)
            edge = jnp.where((lane == p + 5) | (lane == p + 6), turn(jnp.where(first, p3, p4), p + 6), edge)
            out.append(push[old, 0, g, rows, :] + push[old, 1, g, below, :] + push[old, 2, g, above, :]
                       + from_right + from_left)
        strip = (spush[old, 0, o, rows, :] + spush[old, 1, o, below, :] + spush[old, 2, o, above, :]
                 + turn(jnp.where(strip_last, edge, s3), -1) + turn(jnp.where(strip_first, edge, s4), 1))
        return out, strip

    for t in reversed(range(ITERS)):
        new, old = t % 2, (t + 1) % 2

        def spread_out(o, start, t=t, new=new, old=old):
            rows, above, below = where_tile(start)
            if t == ITERS - 1:
                adj = [sen[o * 8 + q, rows, :] for q in range(8)]
                strip = ssen[o, rows, :]
            else:
                adj, strip = gather(o, rows, above, below, old)
                for q in range(8):
                    adjoint[o * 8 + q, rows, :] = adj[q]
            for q in range(8):
                g = o * 8 + q
                grads = [adj[q] * soft[t, a, g, rows, :] for a in range(ACTIONS)]
                for k in range(POINTS):
                    total = grads[0] * chance[k, rows, :]
                    for a in range(1, ACTIONS):
                        total = total + grads[a] * chance[a * POINTS + k, rows, :]
                    push[new, k, g, rows, :] = total
            grads = [strip * ssoft[t, a, o, rows, :] for a in range(ACTIONS)]
            for k in range(POINTS):
                total = grads[0] * schance[k, rows, :]
                for a in range(1, ACTIONS):
                    total = total + grads[a] * schance[a * POINTS + k, rows, :]
                spush[new, k, o, rows, :] = total

        def collect(o, start, t=t):
            rows, above, below = where_tile(start)
            source = sen if t == ITERS - 1 else adjoint
            adj = [source[o * 8 + q, rows, :] for q in range(8)]
            at = slice(start, start + 8)
            for q in range(8):
                g = o * 8 + q
                grads = [adj[q] * soft[t, a, g, rows, :] for a in range(ACTIONS)]
                paysum[g, at, :] += (grads[0] + grads[1]) + (grads[2] + grads[3])
            for a in range(ACTIONS):
                sums = [cgrad[a * POINTS + k, at, :] for k in range(POINTS)]
                total = cgrad[ACTIONS * POINTS + a, at, :]
                for q in range(8):
                    g = o * 8 + q
                    grad = adj[q] * soft[t, a, g, rows, :]
                    total = total + grad
                    near = [val[t][g, rows, :], val[t][g, above, :], val[t][g, below, :],
                            lshift[t, g, rows, :], rshift[t, g, rows, :]]
                    sums = [x + grad * y for x, y in zip(sums, near)]
                for k in range(POINTS):
                    cgrad[a * POINTS + k, at, :] = sums[k]
                cgrad[ACTIONS * POINTS + a, at, :] = total

        def backward_all(o, carry, spread_out=spread_out, collect=collect):
            for start in (-4, 4, 12):
                spread_out(o, start)
            for start in (0, 8):
                collect(o, start)
            return carry

        lax.fori_loop(0, OCT, backward_all, 0)

    def finish(o, carry):
        for start in (0, 8):
            rows, above, below = where_tile(start)
            adj = gather(o, rows, above, below, 0)[0]
            for q in range(8):
                packed[o * 8 + q, start : start + 8, :] = adj[q]
        return carry

    lax.fori_loop(0, OCT, finish, 0)
    snap_ref[...] = packed[...].astype(BF16)
    pay_ref[...] = paysum[...].astype(BF16)
    for j in range(2):
        at = slice(8 * j, 8 * j + 8)
        rows = slice(TOP + 8 * j, TOP + 8 * j + 8)
        for a in range(ACTIONS):
            grads = [cgrad[a * POINTS + k, at, :] for k in range(POINTS)]
            weighted = grads[0] * chance[a * POINTS, rows, :]
            for k in range(1, POINTS):
                weighted = weighted + grads[k] * chance[a * POINTS + k, rows, :]
            for k in range(POINTS):
                cgrad[a * POINTS + k, at, :] = (DECAY * grads[k] - weighted) * slope[a * POINTS + k, at, :]
    number = lax.broadcasted_iota(jnp.int32, (CLASSES, COLS), 0)
    total = jnp.zeros((CLASSES, OUTS), F32)
    which = cls[TOP : TOP + ROWS, :].astype(jnp.int32) - 1
    for i in range(ROWS):
        one_hot = (number == which[i : i + 1]).astype(BF16)
        total = total + dot(one_hot, cgrad[:, i, :].astype(BF16), ((1,), (1,)))
    packed[0, :, :] = jnp.zeros((ROWS, COLS), F32)
    packed[0, 0:CLASSES, 0:OUTS] = total
    parts = [packed[0, 4 * q : 4 * q + 4, :] for q in range(4)]
    sums_ref[...] = (parts[0] + turn(parts[1], 32)) + (turn(parts[2], 64) + turn(parts[3], 96))


def last_kernel(parts_ref, scale_ref, f_ref, h1_ref, h2_ref, w1_ref, w2_ref, w3_ref,
                embed_ref, time_ref, one_ref, two_ref, three_ref, classed, *, factor):
    total = parts_ref[0]
    for i in range(1, parts_ref.shape[0]):
        total = total + parts_ref[i]
    total = total * factor
    for q in range(4):
        classed[4 * q : 4 * q + 4, :] = turn(total, -32 * q)
    sums = classed[:, 0:OUTS]
    f, h1, h2 = f_ref[...], h1_ref[...], h2_ref[...]
    two_grad = split_dot(sums, w3_ref[...], ((1,), (0,))) * (1.0 - h2 * h2)
    one_grad = split_dot(two_grad, w2_ref[...], ((1,), (1,))) * (1.0 - h1 * h1)
    feature_grad = split_dot(one_grad, w1_ref[...], ((1,), (1,)))
    three_ref[...] = split_dot(sums, h2.astype(BF16), ((0,), (0,)))
    two_ref[...] = dot(h1, two_grad, ((0,), (0,)), HIGHEST)
    one_ref[...] = dot(f, one_grad, ((0,), (0,)), HIGHEST)
    embed_ref[...] = feature_grad
    scale = scale_ref[...].astype(F32) * (1.0 / 64.0)
    time_ref[...] = scale[0] * jnp.sum(feature_grad, axis=0)


def shift(x, axis, step):
    size = lax.axis_size(axis)
    pairs = [(i, i + step) for i in range(size) if 0 <= i + step < size]
    return lax.ppermute(x, axis, pairs)


def spread(x, axis, groups=None):
    size = lax.axis_size(axis) if groups is None else len(groups[0])
    copies = jnp.broadcast_to(x[None], (size,) + x.shape)
    return lax.all_to_all(copies, axis, 0, 0, tiled=True, axis_index_groups=groups)


def body(classes, check_index, snapshot, payoff, sensitivity, embed, time_vec, w_one, w_two, w_three):
    sd = jax.ShapeDtypeStruct
    tile = sd((GOALS, ROWS, COLS), BF16)
    marked = (classes + 1).astype(BF16)[None]
    everything = jnp.concatenate([snapshot, payoff, sensitivity, marked], axis=0)
    to_down, to_up = vmem_call(edge_kernel, (tile, tile), [pltpu.VMEM((ROWS, COLS), F32)] * 2)(everything)
    up = shift(to_down, "row", 1)
    down = shift(to_up, "row", -1)

    scale = jnp.broadcast_to(check_index.reshape(1, 1), (1, 64))
    layer = sd((CLASSES, 64), F32)
    square = sd((64, 64), BF16)
    table, feature, one, two, scale, w_one, w_two, w_three = vmem_call(
        table_kernel,
        (sd((72, COLS), F32), layer, layer, layer, sd((1, 64), jnp.int32), square, square, sd((OUTS, 64), BF16)),
        [pltpu.VMEM((32, COLS), F32), pltpu.VMEM((CLASSES, 64), BF16), pltpu.VMEM((1, 64), BF16),
         pltpu.SemaphoreType.DMA((6,))],
        source=pltpu.HBM,
    )(scale, embed, time_vec.reshape(1, -1), w_one, w_two, w_three.T)

    plane = pltpu.VMEM((EXT, COLS), F32)
    edge = sd((OCT + 1, 32, COLS), BF16)
    ext = sd((GOALS, EXT, COLS), F32)
    to_right, to_left, val, rew, sen, cls = vmem_call(
        strip_kernel, (edge, edge, ext, ext, ext, sd((EXT, COLS), F32))
    )(everything, up, down, table)
    left = shift(to_right, "col", 1)
    right = shift(to_left, "col", -1)

    strip = pltpu.VMEM((OCT, EXT, COLS), F32)

    def many(*shape):
        return pltpu.VMEM(shape + (COLS,), F32)

    n = ACTIONS * POINTS
    chance, bonus, mask, slope = vmem_call(
        map_kernel,
        (sd((n, EXT, COLS), F32), sd((ACTIONS, EXT, COLS), F32), sd((EXT, COLS), F32), sd((n, ROWS, COLS), F32)),
    )(cls, table)
    snap, pay, sums = vmem_call(
        main_kernel,
        (tile, tile, sd((4, COLS), F32)),
        [
            many(ITERS - 1, GOALS, EXT), many(ITERS, OCT, EXT), strip, strip, plane,
            many(n, EXT), many(ACTIONS, EXT), plane,
            many(ITERS, ACTIONS, GOALS, EXT), many(ITERS, ACTIONS, OCT, EXT),
            many(ITERS, GOALS, EXT), many(ITERS, GOALS, EXT),
            many(2, POINTS, GOALS, EXT), many(2, POINTS, OCT, EXT), many(GOALS, EXT),
            many(OUTS, ROWS), many(GOALS, ROWS), many(GOALS, ROWS),
        ],
    )(val, rew, sen, cls, chance, bonus, mask, slope, left, right, table)

    rows, cols = lax.axis_size("row"), lax.axis_size("col")
    near = [[r * cols + c + i for r in range(rows) for i in range(2)] for c in range(0, cols, 2)]
    along = [list(range(i, cols, 2)) for i in range(2)]
    sums = jnp.sum(spread(sums, ("row", "col"), near), axis=0)
    parts = spread(sums, "col", along)
    factor = 1.0 / math.sqrt(ROWS * lax.axis_size("row") * COLS * lax.axis_size("col"))

    def last(*refs):
        last_kernel(*refs, factor=factor)

    grads = vmem_call(
        last, (layer, sd((64,), F32), sd((64, 64), F32), sd((64, 64), F32), sd((OUTS, 64), F32)),
        [pltpu.VMEM((CLASSES, COLS), F32)],
    )(parts, scale, feature, one, two, w_one, w_two, w_three)
    return (snap, pay, grads[0], grads[1], grads[2], grads[3], grads[4].T)


def solution(mesh):
    tiled = P(None, "row", "col")
    return jax.shard_map(
        body,
        mesh=mesh,
        in_specs=(P("row", "col"), P(), tiled, tiled, tiled, P(), P(), P(), P(), P()),
        out_specs=(tiled, tiled, P(), P(), P(), P(), P()),
        check_vma=False,
    )
```
